256 devices in a mesh: exp: 64 (over z, x, core), tp: 4 (over y).
Axes of the slice: x: 4, y: 4, z: 8, core: 2. Of those that a mesh axis runs over, the one named last changes fastest.
Arguments:
- tokens: bfloat16 [8192, 3584], P('exp', 'tp'), may hold values from -6 to 6
- expert_ids: int32 [8192, 8], P('exp'), may hold values from 0 to 127, all different within a row; in each aligned block of 128 rows (0 to 127, 128 to 255, ...) at most 10 rows name the same one
- gate_weights: float32 [8192, 8], P('exp'), may hold values from 0.05 to 0.6
- w_gate: bfloat16 [128, 3584, 1024], P('exp', None, 'tp'), may hold values from -0.09375 to 0.09375
- w_up: bfloat16 [128, 3584, 1024], P('exp', None, 'tp'), may hold values from -0.09375 to 0.09375
- w_down: bfloat16 [128, 1024, 3584], P('exp', 'tp'), may hold values from -0.1875 to 0.1875
- s_gate: bfloat16 [3584, 1024], P('exp', 'tp'), may hold values from -0.09375 to 0.09375
- s_up: bfloat16 [3584, 1024], P('exp', 'tp'), may hold values from -0.09375 to 0.09375
- s_down: bfloat16 [1024, 3584], P('tp', 'exp'), may hold values from -0.1875 to 0.1875
Outputs:
- mixed: bfloat16 [8192, 3584], P('exp', 'tp')
The draws below stay inside these ranges and needn't reach their ends.
Inputs may be any that keep to these rules, and one draw needn't show every extreme that they name: `expert_ids`: each row names 8 different experts. In the 128 rows of one index of exp no expert is named by more than 10 rows, and in every draw some expert is named by exactly 10 rows of some index.
All inputs are finite; a program needn't handle non-finite values.
Results may differ from the reference program's by a relative error of at most 0.015.
Values may be sent and summed in bfloat16 or wider, within the bound.
A program may use at most 128 MiB of HBM per device.

```python
import math
import jax
import jax.numpy as jnp
import numpy as np
from jax import lax

D = 3584
HE = 1024
HS = 1024
TOPK = 8
TOK_DEV = 128
EXPERTS = 128
TOKENS = 8192
CAP = 10
N_EXP = 64
N_TP = 4


def steps_of(own_key, shape, pieces, least, largest):
    loudness = 1.0
    for dim, shards_of in pieces:
        heights = jax.random.uniform(jax.random.fold_in(jax.random.fold_in(own_key, 6), dim), (shards_of,), jnp.float32, least / len(pieces), largest / len(pieces))
        loudness = loudness * jnp.repeat(jnp.exp(heights), shape[dim] // shards_of).reshape((-1,) + (1,) * (len(shape) - 1 - dim))
    return loudness


def assign_block(key, own, number, rows, number_of, top, bound, lean):
    ranking = jax.random.permutation(key, number_of)
    crowded, common = portions_of(number_of, rows * top, bound, lean, True), portions_of(number_of, rows * top, bound, lean, False)
    places = jnp.arange(number_of)

    def named(lengths, offset_by):
        used = int((lengths > 0).sum())
        fixed = max(1, used // 4)
        passed = fixed + (places - fixed + offset_by * (used - fixed)) % max(1, number_of - fixed)
        return jnp.zeros((number_of,), jnp.int32).at[ranking[jnp.where(places < fixed, places, passed)]].set(jnp.asarray(lengths, jnp.int32))

    lengths = jnp.where(number % 4 == 0, named(crowded, number // 4), named(common, number - number // 4 - 1))
    mixed = jax.random.permutation(jax.random.fold_in(own, 3), number_of)
    donor, receiver = mixed[0:number_of // 2 * 2:2], mixed[1:number_of // 2 * 2:2]
    slack = jnp.minimum(lengths[donor] - 1, bound - lengths[receiver]) // 2
    slack = jnp.where((donor == ranking[0]) | (receiver == ranking[0]) | (lengths[receiver] == 0), 0, jnp.maximum(slack, 0))
    passed = jax.random.randint(jax.random.fold_in(own, 4), (number_of // 2,), 0, 1 << 20) % (slack + 1)
    lengths = lengths.at[donor].add(-passed).at[receiver].add(passed)
    labels = jnp.searchsorted(jnp.cumsum(lengths), jnp.arange(rows * top), side="right").astype(jnp.int32)
    table = labels.reshape(top, rows).T
    table = table[jax.random.permutation(jax.random.fold_in(own, 1), rows)]
    offset_by = jax.random.randint(jax.random.fold_in(own, 2), (rows, 1), 0, top)
    return jnp.take_along_axis(table, (jnp.arange(top)[None, :] + offset_by) % top, axis=1)


def portions_of(amount, total, most, lean, full):
    weights = [(1 << 20) // math.isqrt(rank ** lean) + 1 for rank in range(1, amount + 1)]
    largest = most if full else min(most, max(-(-total // amount), total * weights[0] // sum(weights)))
    least = 1 if total - largest >= amount - 1 else 0
    given, spare = [largest] + [least] * (amount - 1), total - largest - least * (amount - 1)
    while spare > 0:
        candidates = [i for i in range(1, amount) if given[i] < largest] or [i for i in range(1, amount) if given[i] < most]
        pool, budget = sum([weights[i] for i in candidates]), spare
        for i in candidates:
            more = min(most - given[i], max(1, budget * weights[i] // pool), spare)
            given[i] = given[i] + more
            spare = spare - more
    return np.array(given)


def noise(own_key, extent, width, limit, cuts=(), held_as=jnp.bfloat16):
    values = width * jax.random.normal(own_key, extent, jnp.float32)
    if cuts:
        values = values * steps_of(own_key, extent, cuts, -0.22, 0.18)
    return jnp.clip(values, -limit, limit).astype(held_as)


def setup_inputs(seed: int = 0) -> dict:
    seeds = jax.random.split(jax.random.key(seed), 10)
    tokens = noise(seeds[0], (TOKENS, D), 1.0, 6.0, ((0, 64), (1, 4)))
    expert_ids_keys = jax.random.split(jax.random.fold_in(seeds[1], 1), TOKENS // TOK_DEV)
    expert_ids_turns = jax.random.permutation(jax.random.fold_in(seeds[1], 3), TOKENS // TOK_DEV)
    expert_ids = jax.vmap(lambda own, number: assign_block(jax.random.fold_in(seeds[1], 2), own, number, TOK_DEV, EXPERTS, TOPK, CAP, 1))(expert_ids_keys, expert_ids_turns).reshape((TOKENS, TOPK))
    gate_weights = jnp.clip(0.05 + 0.55 * jax.random.uniform(seeds[2], (TOKENS, TOPK), jnp.float32) ** steps_of(seeds[2], (TOKENS, TOPK), ((0, 64),), -0.2, 0.2), 0.05, 0.6)
    w_gate = noise(seeds[3], (EXPERTS, D, HE), D ** -0.5, 0.09375, ((0, 64), (2, 4)))
    w_up = noise(seeds[4], (EXPERTS, D, HE), D ** -0.5, 0.09375, ((0, 64), (2, 4)))
    w_down = noise(seeds[5], (EXPERTS, HE, D), HE ** -0.5, 0.1875, ((0, 64), (1, 4)))
    s_gate = noise(seeds[6], (D, HS), D ** -0.5, 0.09375, ((0, 64), (1, 4)))
    s_up = noise(seeds[7], (D, HS), D ** -0.5, 0.09375, ((0, 64), (1, 4)))
    s_down = noise(seeds[8], (HS, D), HS ** -0.5, 0.1875, ((0, 4), (1, 64)))
    return {"tokens": tokens, "expert_ids": expert_ids, "gate_weights": gate_weights, "w_gate": w_gate, "w_up": w_up, "w_down": w_down, "s_gate": s_gate, "s_up": s_up, "s_down": s_down}


def reference(tokens, expert_ids, gate_weights, w_gate, w_up, w_down, s_gate, s_up, s_down):
    block_rows = TOK_DEV * TOPK
    blocks = expert_ids.reshape(N_EXP, block_rows)
    columns = jnp.arange(EXPERTS, dtype=jnp.int32)
    onehot = (blocks[:, :, None] == columns[None, None, :]).astype(jnp.int32)
    position = jnp.sum((jnp.cumsum(onehot, axis=1) - onehot) * onehot, axis=2)
    source = jnp.arange(N_EXP, dtype=jnp.int32)[:, None]
    slot_of = ((blocks * N_EXP + source) * CAP + position).astype(jnp.int32).reshape(TOKENS, TOPK)
    entries = jnp.arange(TOKENS * TOPK, dtype=jnp.int32)
    filler = jnp.full((EXPERTS * N_EXP * CAP,), -1, jnp.int32).at[slot_of.reshape(-1)].set(entries)
    present = filler >= 0
    token_of = jnp.where(present, filler // TOPK, 0).astype(jnp.int32)
    block_hidden = HE // N_TP

    def one_expert(packed):
        index, mask, gate_matrix, up_matrix, down_matrix = packed
        rows = jnp.where(mask[:, None], tokens[index], jnp.zeros((), tokens.dtype))
        gate = jnp.dot(rows, gate_matrix, preferred_element_type=jnp.float32)
        upper = jnp.dot(rows, up_matrix, preferred_element_type=jnp.float32)
        hidden = (jax.nn.silu(gate) * upper).astype(jnp.bfloat16)
        total = jnp.zeros((index.shape[0], D), jnp.float32)
        for block in range(N_TP):
            start = block * block_hidden
            piece = jnp.dot(hidden[:, start:start + block_hidden], down_matrix[start:start + block_hidden], preferred_element_type=jnp.float32)
            total = total + lax.optimization_barrier(piece.astype(jnp.bfloat16)).astype(jnp.float32)
        return total

    expert_out = lax.map(one_expert, (token_of.reshape(EXPERTS, N_EXP * CAP), present.reshape(EXPERTS, N_EXP * CAP), w_gate, w_up, w_down))
    expert_out = expert_out.reshape(EXPERTS * N_EXP * CAP, D)
    routed = jnp.zeros((TOKENS, D), jnp.float32)
    for choose in range(TOPK):
        routed = routed + gate_weights[:, choose:choose + 1] * expert_out[slot_of[:, choose]]
    shared_gate = jnp.dot(tokens, s_gate, preferred_element_type=jnp.float32)
    shared_up = jnp.dot(tokens, s_up, preferred_element_type=jnp.float32)
    shared_hidden = (jax.nn.silu(shared_gate) * shared_up).astype(jnp.bfloat16)
    shared = jnp.dot(shared_hidden, s_down, preferred_element_type=jnp.float32)
    return (routed + shared).astype(jnp.bfloat16)
```

```python
import functools

import jax
import jax.numpy as jnp
from jax import lax
from jax.experimental import pallas as pl
from jax.experimental.pallas import tpu as pltpu
from jax.sharding import PartitionSpec as P

MESH = pl.DeviceIdType.MESH
NY = 4
NC = 2
LANES = 128


def dims_of(exp_count):
    nz, nx = {64: (8, 4), 4: (2, 1)}[exp_count]
    return nz, nx


def routed_kernel(
    nz, nd, cap, tok, top, chunks, hid,
    tokens_ref, ids_ref, wts_ref, wg_hbm, wu_hbm, wd_hbm,
    out_ref,
    wg, wu, wd, meta_src, meta, sel, cmb_rows, cmb, held, packed, rows, gate, upper, hidden,
    outs, back, part, home,
    load_sem, wd_send, wd_recv, meta_send, meta_recv, z_send, z_recv, x_send, x_recv,
    y_send, y_recv, b_send, b_recv, h_send, h_recv,
):
    quarter = chunks * LANES
    grp = nz * cap
    f32, bf16 = jnp.float32, jnp.bfloat16
    exp = lax.axis_index("exp")
    y = lax.axis_index("tp")
    z = exp // nd
    d = exp % nd
    right = (y + 1) % NY
    left = (y + NY - 1) % NY
    across = (y + 2) % NY

    def z_peer(j):
        return (((z + j) % nz) * nd + d, y)

    def d_peer(r):
        return (z * nd + (d + r) % nd, y)

    def y_peer(q):
        return (exp, q)

    def send(src, dst, ss, rs, dev):
        pltpu.make_async_remote_copy(
            src_ref=src, dst_ref=dst, send_sem=ss, recv_sem=rs, device_id=dev, device_id_type=MESH
        ).start()

    def wait(ref, sem):
        pltpu.make_async_copy(ref, ref, sem).wait()

    load_g = pltpu.make_async_copy(wg_hbm, wg, load_sem.at[0])
    load_u = pltpu.make_async_copy(wu_hbm, wu, load_sem.at[1])
    load_d = pltpu.make_async_copy(wd_hbm.at[:, :, pl.ds(y * quarter, quarter)], wd.at[0], load_sem.at[2])
    load_g.start()
    load_u.start()
    load_d.start()

    barrier = pltpu.get_barrier_semaphore()
    for j in range(1, nz):
        pl.semaphore_signal(barrier, inc=1, device_id=z_peer(j), device_id_type=MESH)
    for r in range(1, nd):
        pl.semaphore_signal(barrier, inc=1, device_id=d_peer(r), device_id_type=MESH)
    for q in (left, right, across):
        pl.semaphore_signal(barrier, inc=1, device_id=y_peer(q), device_id_type=MESH)

    experts = nz * nd * 2
    lane = lax.broadcasted_iota(jnp.int32, (tok, experts), 1)
    named = jnp.zeros((tok, experts), f32)
    weight = jnp.zeros((tok, experts), f32)
    for k in range(top):
        hit = ids_ref[:, k:k + 1] == lane
        named = named + jnp.where(hit, 1.0, 0.0)
        weight = weight + jnp.where(hit, wts_ref[:, k:k + 1], 0.0)
    named_t = named.T
    before = lax.broadcasted_iota(jnp.int32, (tok, tok), 0) < lax.broadcasted_iota(jnp.int32, (tok, tok), 1)
    rank = jnp.dot(
        named_t.astype(bf16), jnp.where(before, 1.0, 0.0).astype(bf16), preferred_element_type=f32
    )
    meta_src[0] = jnp.where(named_t > 0.5, rank, -1.0)
    meta_src[1] = weight.T
    plane = 2 * nd

    pl.semaphore_wait(barrier, nz - 1 + nd - 1 + 3)

    for j in range(1, nz):
        zj = (z + j) % nz
        send(
            meta_src.at[:, pl.ds(pl.multiple_of(zj * plane, plane), plane), :],
            meta.at[:, :, pl.ds(j * tok, tok)],
            meta_send, meta_recv, z_peer(j),
        )
    meta[:, :, 0:tok] = meta_src[:, pl.ds(pl.multiple_of(z * plane, plane), plane), :]

    def send_tokens(k, carry):
        cols = pl.ds(pl.multiple_of(k * LANES, LANES), LANES)
        for j in range(1, nz):
            send(tokens_ref.at[:, cols], held.at[k, j], z_send.at[k], z_recv.at[k], z_peer(j))
        held[k, 0] = tokens_ref[:, cols]
        return carry

    lax.fori_loop(0, chunks, send_tokens, 0)

    for slot, q in ((1, right), (2, left), (3, across)):
        send(
            wd_hbm.at[:, :, pl.ds(pl.multiple_of(q * quarter, LANES), quarter)],
            wd.at[slot], wd_send.at[slot - 1], wd_recv.at[slot - 1], y_peer(q),
        )

    wait(meta.at[:, :, pl.ds(tok, (nz - 1) * tok)], meta_recv)

    row = lax.broadcasted_iota(jnp.int32, (grp, nz * tok), 0)
    col = lax.broadcasted_iota(jnp.int32, (grp, nz * tok), 1)
    wanted = jnp.where(row % nz == col // tok, row // nz, -5).astype(f32)

    def build(g, carry):
        r = g // 2
        index = ((d + r) % nd) * 2 + g % 2
        hit = meta[0, pl.ds(index, 1), :] == wanted
        sel[g] = jnp.where(hit, 1.0, 0.0).astype(bf16)
        cmb_rows[pl.ds(pl.multiple_of(g * grp, 16), grp), :] = jnp.where(
            hit, meta[1, pl.ds(index, 1), :], 0.0
        ).astype(bf16)
        return carry

    lax.fori_loop(0, 2 * nd, build, 0)

    gate[...] = jnp.zeros_like(gate)
    upper[...] = jnp.zeros_like(upper)

    def select(k, r):
        picked = jnp.dot(
            sel[pl.ds(2 * r, 2)].reshape(2 * grp, nz * tok),
            held[k].reshape(nz * tok, LANES),
            preferred_element_type=f32,
        )
        return picked.astype(bf16).reshape(2, grp, LANES)

    def stage_a(k):
        wait(held.at[k, pl.ds(1, nz - 1)], z_recv.at[k])

        def one(r, carry):
            packed[k, r] = select(k, r)
            send(packed.at[k, r], rows.at[0, k, :, r], x_send.at[k], x_recv.at[k], d_peer(r))
            return carry

        lax.fori_loop(1, nd, one, 0)
        rows[0, k, :, 0] = select(k, 0)

    def stage_b(k):
        wait(rows.at[0, k, :, pl.ds(1, nd - 1)], x_recv.at[k])
        send(rows.at[0, k], rows.at[1, k], y_send.at[0, k], y_recv.at[0, k], y_peer(right))
        send(rows.at[0, k], rows.at[2, k], y_send.at[1, k], y_recv.at[1, k], y_peer(left))

    halves = nd // 2

    def accumulate(k, slots):
        def one(i, carry):
            e = i // 2
            h = i % 2
            g = gate[e, h]
            u = upper[e, h]
            for s, q in slots:
                x = rows[s, k, e, pl.ds(h * halves, halves)].reshape(halves * grp, LANES)
                at = pl.ds(pl.multiple_of(q * quarter + k * LANES, LANES), LANES)
                g = g + jnp.dot(x, wg[e, at, :], preferred_element_type=f32)
                u = u + jnp.dot(x, wu[e, at, :], preferred_element_type=f32)
            gate[e, h] = g
            upper[e, h] = u
            return carry

        lax.fori_loop(0, 4, one, 0)

    def stage_c(k):
        wait(rows.at[1, k], y_recv.at[0, k])
        send(rows.at[1, k, 0], rows.at[3, k, 0], y_send.at[2, k], y_recv.at[2, k], y_peer(right))
        wait(rows.at[2, k], y_recv.at[1, k])
        send(rows.at[2, k, 1], rows.at[3, k, 1], y_send.at[3, k], y_recv.at[3, k], y_peer(left))
        accumulate(k, ((0, y), (1, left), (2, right)))

    def stage_d(k):
        wait(rows.at[3, k, 0], y_recv.at[2, k])
        wait(rows.at[3, k, 1], y_recv.at[3, k])
        accumulate(k, ((3, across),))

    load_g.wait()
    load_u.wait()

    lag_b, lag_c, lag_d = 1, 2, 4

    def step(i, carry):
        @pl.when(i < chunks)
        def _():
            stage_a(i)

        @pl.when((i >= lag_b) & (i < chunks + lag_b))
        def _():
            stage_b(i - lag_b)

        @pl.when((i >= lag_c) & (i < chunks + lag_c))
        def _():
            stage_c(i - lag_c)

        @pl.when(i >= lag_d)
        def _():
            stage_d(i - lag_d)

        return carry

    lax.fori_loop(0, chunks + lag_d, step, 0)

    half_rows = halves * grp
    for e in range(2):
        for h in range(2):
            g = gate[e, h]
            hidden[0, e, h * half_rows:(h + 1) * half_rows, :] = (
                g / (1.0 + jnp.exp(-g)) * upper[e, h]
            ).astype(bf16)
        u = chunks + e
        send(hidden.at[0, e], hidden.at[1, e], y_send.at[0, u], y_recv.at[0, u], y_peer(right))
        send(hidden.at[0, e], hidden.at[2, e], y_send.at[1, u], y_recv.at[1, u], y_peer(left))

    def turn(a, carry):
        block = pl.ds(pl.multiple_of(a * LANES, LANES), LANES)
        cmb[:, block] = cmb_rows[block, :].astype(f32).T.astype(bf16)
        return carry

    lax.fori_loop(0, 2 * nd * grp // LANES, turn, 0)

    low, high = pl.ds(0, half_rows), pl.ds(half_rows, half_rows)
    for e in range(2):
        u = chunks + e
        wait(hidden.at[1, e], y_recv.at[0, u])
        send(hidden.at[1, e, low], hidden.at[3, e, low], y_send.at[2, u], y_recv.at[2, u], y_peer(right))
        wait(hidden.at[2, e], y_recv.at[1, u])
        send(hidden.at[2, e, high], hidden.at[3, e, high], y_send.at[3, u], y_recv.at[3, u], y_peer(left))
    load_d.wait()
    for slot in (1, 2, 3):
        wait(wd.at[slot], wd_recv.at[slot - 1])
    for e in range(2):
        u = chunks + e
        wait(hidden.at[3, e, low], y_recv.at[2, u])
        wait(hidden.at[3, e, high], y_recv.at[3, u])

    def stage_e(k):
        cols = pl.ds(pl.multiple_of(k * LANES, LANES), LANES)
        for e in range(2):
            total = jnp.zeros((nd * grp, LANES), f32)
            for s in range(NY):
                total = total + jnp.dot(hidden[s, e], wd[s, e, :, cols], preferred_element_type=f32)
            value = total.astype(bf16).reshape(nd, grp, LANES)
            outs[k, :, e] = value
            back[k, 0, e] = value[0]

        def one(r, carry):
            send(outs.at[k, r], back.at[k, r], b_send.at[k], b_recv.at[k], d_peer(nd - r))
            return carry

        lax.fori_loop(1, nd, one, 0)

    def stage_f(k):
        wait(back.at[k, pl.ds(1, nd - 1)], b_recv.at[k])
        per = nz // 2
        for i in range(2):
            value = jnp.dot(
                cmb[i * per * tok:(i + 1) * per * tok, :],
                back[k].reshape(2 * nd * grp, LANES),
                preferred_element_type=f32,
            ).astype(bf16).reshape(per, tok, LANES)
            part[k, i * per:(i + 1) * per] = value
            for j in range(max(1, i * per), (i + 1) * per):
                send(part.at[k, j], home.at[k, j], h_send.at[k], h_recv.at[k], z_peer(nz - j))

    def stage_g(k):
        wait(home.at[k, pl.ds(1, nz - 1)], h_recv.at[k])
        total = part[k, 0].astype(f32)
        for j in range(1, nz):
            total = total + home[k, j].astype(f32)
        out_ref[:, pl.ds(pl.multiple_of(k * LANES, LANES), LANES)] = total

    lag_f, lag_g = 1, 3

    def step_back(i, carry):
        @pl.when(i < chunks)
        def _():
            stage_e(i)

        @pl.when((i >= lag_f) & (i < chunks + lag_f))
        def _():
            stage_f(i - lag_f)

        @pl.when(i >= lag_g)
        def _():
            stage_g(i - lag_g)

        return carry

    lax.fori_loop(0, chunks + lag_g, step_back, 0)

    wait(meta.at[:, :, pl.ds(tok, (nz - 1) * tok)], meta_send)
    for slot in (1, 2, 3):
        wait(wd.at[slot], wd_send.at[slot - 1])

    def drain(k, carry):
        wait(held.at[k, pl.ds(1, nz - 1)], z_send.at[k])
        wait(packed.at[k, pl.ds(1, nd - 1)], x_send.at[k])
        wait(rows.at[0, k], y_send.at[0, k])
        wait(rows.at[0, k], y_send.at[1, k])
        wait(rows.at[1, k, 0], y_send.at[2, k])
        wait(rows.at[2, k, 1], y_send.at[3, k])
        wait(outs.at[k, pl.ds(1, nd - 1)], b_send.at[k])
        wait(part.at[k, pl.ds(1, nz - 1)], h_send.at[k])
        return carry

    lax.fori_loop(0, chunks, drain, 0)
    for e in range(2):
        u = chunks + e
        wait(hidden.at[0, e], y_send.at[0, u])
        wait(hidden.at[0, e], y_send.at[1, u])
        wait(hidden.at[1, e, low], y_send.at[2, u])
        wait(hidden.at[2, e, high], y_send.at[3, u])


def routed(tokens, expert_ids, gate_weights, w_gate, w_up, w_down, cap):
    nz, nx = dims_of(lax.axis_size("exp"))
    nd = nx * NC
    tok, quarter = tokens.shape
    top = expert_ids.shape[1]
    width, hid = w_gate.shape[1:]
    chunks = quarter // LANES
    grp = nz * cap
    f32, bf16 = jnp.float32, jnp.bfloat16
    dma = pltpu.SemaphoreType.DMA
    vm = pltpu.VMEM
    slots = 2 * nd * grp
    hbm = pl.BlockSpec(memory_space=pl.ANY)
    inside = pl.BlockSpec(memory_space=pltpu.VMEM)
    return pl.pallas_call(
        functools.partial(routed_kernel, nz, nd, cap, tok, top, chunks, hid),
        out_shape=jax.ShapeDtypeStruct((tok, quarter), f32),
        in_specs=[inside, inside, inside, hbm, hbm, hbm],
        out_specs=inside,
        scratch_shapes=[
            vm((2, width, hid), bf16),
            vm((2, width, hid), bf16),
            vm((NY, 2, hid, quarter), bf16),
            vm((2, 2 * nz * nd, tok), f32),
            vm((2, 2 * nd, nz * tok), f32),
            vm((2 * nd, grp, nz * tok), bf16),
            vm((slots, nz * tok), bf16),
            vm((nz * tok, slots), bf16),
            vm((chunks, nz, tok, LANES), bf16),
            vm((chunks, nd, 2, grp, LANES), bf16),
            vm((NY, chunks, 2, nd, grp, LANES), bf16),
            vm((2, 2, nd // 2 * grp, hid), f32),
            vm((2, 2, nd // 2 * grp, hid), f32),
            vm((NY, 2, nd * grp, hid), bf16),
            vm((chunks, nd, 2, grp, LANES), bf16),
            vm((chunks, nd, 2, grp, LANES), bf16),
            vm((chunks, nz, tok, LANES), bf16),
            vm((chunks, nz, tok, LANES), bf16),
            dma((3,)), dma((3,)), dma((3,)), dma, dma,
            dma((chunks,)), dma((chunks,)), dma((chunks,)), dma((chunks,)),
            dma((4, chunks + 2)), dma((4, chunks + 2)),
            dma((chunks,)), dma((chunks,)), dma((chunks,)), dma((chunks,)),
        ],
        compiler_params=pltpu.CompilerParams(
            collective_id=0, has_side_effects=True, vmem_limit_bytes=60 * 1024 * 1024
        ),
        cost_estimate=pl.CostEstimate(
            flops=2 * slots * width * hid * 3, bytes_accessed=6 * width * hid * 2, transcendentals=slots * hid
        ),
        name="routed",
    )(tokens, expert_ids, gate_weights, w_gate, w_up, w_down)


def body(tokens, expert_ids, gate_weights, w_gate, w_up, w_down, s_gate, s_up, s_down):
    exp_count = lax.axis_size("exp")
    tok_count, top_count = expert_ids.shape
    experts = w_gate.shape[0] * exp_count
    capacity = max(2, 5 * tok_count * top_count // (4 * experts))
    units = s_gate.shape[1]
    whole = lax.all_gather(tokens, "tp", axis=1, tiled=True)
    shard = jnp.concatenate([s_gate, s_up, s_down.T], axis=1)
    shared_w = lax.all_gather(shard, "exp", axis=0, tiled=True)
    routed_sum = routed(tokens, expert_ids, gate_weights, w_gate, w_up, w_down, capacity)
    both = jnp.dot(whole, shared_w[:, :2 * units], preferred_element_type=jnp.float32)
    shared_hidden = (jax.nn.silu(both[:, :units]) * both[:, units:]).astype(jnp.bfloat16)
    shared_part = lax.dot_general(
        shared_hidden, shared_w[:, 2 * units:], (((1,), (1,)), ((), ())), preferred_element_type=jnp.float32
    )
    shared_sum = lax.psum_scatter(
        shared_part.astype(jnp.bfloat16), "tp", scatter_dimension=1, tiled=True
    ).astype(jnp.float32)
    return (shared_sum + routed_sum).astype(jnp.bfloat16)


def solution(mesh):
    return jax.shard_map(
        body,
        mesh=mesh,
        in_specs=(
            P("exp", "tp"),
            P("exp", None),
            P("exp", None),
            P("exp", None, "tp"),
            P("exp", None, "tp"),
            P("exp", "tp", None),
            P("exp", "tp"),
            P("exp", "tp"),
            P("tp", "exp"),
        ),
        out_specs=P("exp", "tp"),
        check_vma=False,
    )
```

```python
import functools

import jax
import jax.numpy as jnp
from jax import lax
from jax.experimental import pallas as pl
from jax.experimental.pallas import tpu as pltpu
from jax.sharding import PartitionSpec as P

MESH = pl.DeviceIdType.MESH
NY = 4
NC = 2
LANES = 128


def dims_of(exp_count):
    nz, nx = {64: (8, 4), 4: (2, 1)}[exp_count]
    return nz, nx


def layer_kernel(
    nz, nd, cap, tok, top, chunks, hid,
    tokens_ref, ids_ref, wts_ref, wg_hbm, wu_hbm, wd_hbm, shard_ref,
    out_ref,
    wg, wu, wd, meta_src, meta, sel, cmb_rows, cmb, held, packed, rows, gate, upper, hidden,
    outs, back, part, home,
    spread, shards, tokens_y, padded, pieces, pieces_y,
    load_sem, wd_send, wd_recv, meta_send, meta_recv, z_send, z_recv, x_send, x_recv,
    y_send, y_recv, b_send, b_recv, h_send, h_recv,
    sz_send, sz_recv, sx_send, sx_recv, sc_send, sc_recv, t_send, t_recv, p_send, p_recv,
):
    quarter = chunks * LANES
    grp = nz * cap
    f32, bf16 = jnp.float32, jnp.bfloat16
    exp = lax.axis_index("exp")
    y = lax.axis_index("tp")
    z = exp // nd
    d = exp % nd
    right = (y + 1) % NY
    left = (y + NY - 1) % NY
    across = (y + 2) % NY

    def z_peer(j):
        return (((z + j) % nz) * nd + d, y)

    def d_peer(r):
        return (z * nd + (d + r) % nd, y)

    def y_peer(q):
        return (exp, q)

    nx = nd // NC
    x = d // NC
    core = d % NC

    def d_of(r, c):
        return ((x + nx - r) % nx) * NC + c

    def send(src, dst, ss, rs, dev):
        pltpu.make_async_remote_copy(
            src_ref=src, dst_ref=dst, send_sem=ss, recv_sem=rs, device_id=dev, device_id_type=MESH
        ).start()

    def wait(ref, sem):
        pltpu.make_async_copy(ref, ref, sem).wait()

    load_g = pltpu.make_async_copy(wg_hbm, wg, load_sem.at[0])
    load_u = pltpu.make_async_copy(wu_hbm, wu, load_sem.at[1])
    load_d = pltpu.make_async_copy(wd_hbm.at[:, :, pl.ds(y * quarter, quarter)], wd.at[0], load_sem.at[2])
    load_g.start()
    load_u.start()
    load_d.start()

    barrier = pltpu.get_barrier_semaphore()
    for j in range(1, nz):
        pl.semaphore_signal(barrier, inc=1, device_id=z_peer(j), device_id_type=MESH)
    for r in range(1, nd):
        pl.semaphore_signal(barrier, inc=1, device_id=d_peer(r), device_id_type=MESH)
    for q in (left, right, across):
        pl.semaphore_signal(barrier, inc=1, device_id=y_peer(q), device_id_type=MESH)

    experts = nz * nd * 2
    lane = lax.broadcasted_iota(jnp.int32, (tok, experts), 1)
    named = jnp.zeros((tok, experts), f32)
    weight = jnp.zeros((tok, experts), f32)
    for k in range(top):
        hit = ids_ref[:, k:k + 1] == lane
        named = named + jnp.where(hit, 1.0, 0.0)
        weight = weight + jnp.where(hit, wts_ref[:, k:k + 1], 0.0)
    named_t = named.T
    before = lax.broadcasted_iota(jnp.int32, (tok, tok), 0) < lax.broadcasted_iota(jnp.int32, (tok, tok), 1)
    rank = jnp.dot(
        named_t.astype(bf16), jnp.where(before, 1.0, 0.0).astype(bf16), preferred_element_type=f32
    )
    meta_src[0] = jnp.where(named_t > 0.5, rank, -1.0)
    meta_src[1] = weight.T
    plane = 2 * nd

    pl.semaphore_wait(barrier, nz - 1 + nd - 1 + 3)

    for j in range(1, nz):
        zj = (z + j) % nz
        send(
            meta_src.at[:, pl.ds(pl.multiple_of(zj * plane, plane), plane), :],
            meta.at[:, :, pl.ds(j * tok, tok)],
            meta_send, meta_recv, z_peer(j),
        )
    meta[:, :, 0:tok] = meta_src[:, pl.ds(pl.multiple_of(z * plane, plane), plane), :]

    y_slots = ((1, right), (2, left), (3, across))
    for slot, q in y_slots:
        send(tokens_ref, tokens_y.at[slot - 1], t_send.at[slot - 1], t_recv.at[slot - 1], y_peer(q))

    def send_tokens(k, carry):
        cols = pl.ds(pl.multiple_of(k * LANES, LANES), LANES)
        for j in range(1, nz):
            send(tokens_ref.at[:, cols], held.at[k, j], z_send.at[k], z_recv.at[k], z_peer(j))
        held[k, 0] = tokens_ref[:, cols]
        return carry

    lax.fori_loop(0, chunks, send_tokens, 0)

    for j in range(1, nz):
        send(shard_ref, shards.at[:, j, d], sz_send, sz_recv, z_peer(j))
    shards[:, 0, d] = shard_ref[...]

    for slot, q in y_slots:
        send(
            wd_hbm.at[:, :, pl.ds(pl.multiple_of(q * quarter, LANES), quarter)],
            wd.at[slot], wd_send.at[slot - 1], wd_recv.at[slot - 1], y_peer(q),
        )

    wait(meta.at[:, :, pl.ds(tok, (nz - 1) * tok)], meta_recv)

    row = lax.broadcasted_iota(jnp.int32, (grp, nz * tok), 0)
    col = lax.broadcasted_iota(jnp.int32, (grp, nz * tok), 1)
    wanted = jnp.where(row % nz == col // tok, row // nz, -5).astype(f32)

    def build(g, carry):
        r = g // 2
        index = ((d + r) % nd) * 2 + g % 2
        hit = meta[0, pl.ds(index, 1), :] == wanted
        sel[g] = jnp.where(hit, 1.0, 0.0).astype(bf16)
        cmb_rows[pl.ds(pl.multiple_of(g * grp, 16), grp), :] = jnp.where(
            hit, meta[1, pl.ds(index, 1), :], 0.0
        ).astype(bf16)
        return carry

    lax.fori_loop(0, 2 * nd, build, 0)

    gate[...] = jnp.zeros_like(gate)
    upper[...] = jnp.zeros_like(upper)

    def select(k, r):
        picked = jnp.dot(
            sel[pl.ds(2 * r, 2)].reshape(2 * grp, nz * tok),
            held[k].reshape(nz * tok, LANES),
            preferred_element_type=f32,
        )
        return picked.astype(bf16).reshape(2, grp, LANES)

    def stage_a(k):
        wait(held.at[k, pl.ds(1, nz - 1)], z_recv.at[k])

        def one(r, carry):
            packed[k, r] = select(k, r)
            send(packed.at[k, r], rows.at[0, k, :, r], x_send.at[k], x_recv.at[k], d_peer(r))
            return carry

        lax.fori_loop(1, nd, one, 0)
        rows[0, k, :, 0] = select(k, 0)

    def stage_b(k):
        wait(rows.at[0, k, :, pl.ds(1, nd - 1)], x_recv.at[k])
        send(rows.at[0, k], rows.at[1, k], y_send.at[0, k], y_recv.at[0, k], y_peer(right))
        send(rows.at[0, k], rows.at[2, k], y_send.at[1, k], y_recv.at[1, k], y_peer(left))

    halves = nd // 2

    def accumulate(k, slots):
        def one(i, carry):
            e = i // 2
            h = i % 2
            g = gate[e, h]
            u = upper[e, h]
            for s, q in slots:
                x = rows[s, k, e, pl.ds(h * halves, halves)].reshape(halves * grp, LANES)
                at = pl.ds(pl.multiple_of(q * quarter + k * LANES, LANES), LANES)
                g = g + jnp.dot(x, wg[e, at, :], preferred_element_type=f32)
                u = u + jnp.dot(x, wu[e, at, :], preferred_element_type=f32)
            gate[e, h] = g
            upper[e, h] = u
            return carry

        lax.fori_loop(0, 4, one, 0)

    def stage_c(k):
        wait(rows.at[1, k], y_recv.at[0, k])
        send(rows.at[1, k, 0], rows.at[3, k, 0], y_send.at[2, k], y_recv.at[2, k], y_peer(right))
        wait(rows.at[2, k], y_recv.at[1, k])
        send(rows.at[2, k, 1], rows.at[3, k, 1], y_send.at[3, k], y_recv.at[3, k], y_peer(left))
        accumulate(k, ((0, y), (1, left), (2, right)))

    def stage_d(k):
        wait(rows.at[3, k, 0], y_recv.at[2, k])
        wait(rows.at[3, k, 1], y_recv.at[3, k])
        accumulate(k, ((3, across),))

    def shards_in_plane():
        wait(shards.at[:, pl.ds(1, nz - 1), d], sz_recv)
        mine = shards.at[:, :, d]
        for r in range(1, nx):
            send(mine, mine, sx_send.at[r - 1], sx_recv.at[r - 1], (z * nd + ((x + r) % nx) * NC + core, y))
        send(mine, mine, sc_send.at[0], sc_recv.at[0], (z * nd + x * NC + 1 - core, y))

    def shards_in_chip():
        for r in range(1, nx):
            block = shards.at[:, :, d_of(r, core)]
            wait(block, sx_recv.at[r - 1])
            send(block, block, sc_send.at[r], sc_recv.at[r], (z * nd + x * NC + 1 - core, y))

    rp = shard_ref.shape[1]
    rs = quarter * NY // (nz * nd)
    per_quarter = quarter // rs
    run = min(per_quarter, nd)

    def spread_matrix():
        into = lax.broadcasted_iota(jnp.int32, spread.shape, 1)
        at = lax.broadcasted_iota(jnp.int32, spread.shape, 0)
        inner = into % rp
        spread[...] = jnp.where((inner < rs) & (at == into // rp * rs + inner), 1.0, 0.0).astype(bf16)

    def block_of(m, q, i):
        first = q * per_quarter + i * run
        zr = (z + nz - first // nd) % nz
        return shards[m, zr, pl.ds(first % nd, run)].reshape(run * rp, hid)

    def shared_expert():
        for r in range(nx):
            wait(shards.at[:, :, d_of(r, 1 - core)], sc_recv.at[r])
        s_gate = jnp.zeros((tok, hid), f32)
        s_upper = jnp.zeros((tok, hid), f32)
        for slot, q in ((0, y), (1, left), (2, right), (3, across)):
            if slot:
                wait(tokens_y.at[slot - 1], t_recv.at[slot - 1])
            source = tokens_y[slot - 1] if slot else tokens_ref[...]
            padded[...] = jnp.dot(source, spread[...], preferred_element_type=f32).astype(bf16)
            for i in range(per_quarter // run):
                lhs = padded[:, i * run * rp:(i + 1) * run * rp]
                s_gate = s_gate + jnp.dot(lhs, block_of(0, q, i), preferred_element_type=f32)
                s_upper = s_upper + jnp.dot(lhs, block_of(1, q, i), preferred_element_type=f32)
        act = (s_gate / (1.0 + jnp.exp(-s_gate)) * s_upper).astype(bf16)
        across_rows = (((1,), (1,)), ((), ()))
        for slot, q in ((1, right), (2, left), (3, across), (0, y)):
            for i in range(per_quarter // run):
                padded[:, i * run * rp:(i + 1) * run * rp] = lax.dot_general(
                    act, block_of(2, q, i), across_rows, preferred_element_type=f32
                ).astype(bf16)
            pieces[slot] = lax.dot_general(
                padded[...], spread[...], across_rows, preferred_element_type=f32
            ).astype(bf16)
            if slot:
                send(pieces.at[slot], pieces_y.at[slot - 1], p_send.at[slot - 1], p_recv.at[slot - 1], y_peer(q))

    load_g.wait()
    load_u.wait()

    lag_b, lag_c, lag_d = 1, 2, 4

    def step(i, carry):
        @pl.when(i < chunks)
        def _():
            stage_a(i)

        @pl.when(i == 3)
        def _():
            shards_in_plane()

        @pl.when(i == chunks)
        def _():
            spread_matrix()
            shards_in_chip()

        @pl.when((i >= lag_b) & (i < chunks + lag_b))
        def _():
            stage_b(i - lag_b)

        @pl.when((i >= lag_c) & (i < chunks + lag_c))
        def _():
            stage_c(i - lag_c)

        @pl.when(i >= lag_d)
        def _():
            stage_d(i - lag_d)

        return carry

    lax.fori_loop(0, chunks + lag_d, step, 0)

    half_rows = halves * grp
    for e in range(2):
        for h in range(2):
            g = gate[e, h]
            hidden[0, e, h * half_rows:(h + 1) * half_rows, :] = (
                g / (1.0 + jnp.exp(-g)) * upper[e, h]
            ).astype(bf16)
        u = chunks + e
        send(hidden.at[0, e], hidden.at[1, e], y_send.at[0, u], y_recv.at[0, u], y_peer(right))
        send(hidden.at[0, e], hidden.at[2, e], y_send.at[1, u], y_recv.at[1, u], y_peer(left))

    shared_expert()

    def turn(a, carry):
        block = pl.ds(pl.multiple_of(a * LANES, LANES), LANES)
        cmb[:, block] = cmb_rows[block, :].astype(f32).T.astype(bf16)
        return carry

    lax.fori_loop(0, 2 * nd * grp // LANES, turn, 0)

    low, high = pl.ds(0, half_rows), pl.ds(half_rows, half_rows)
    for e in range(2):
        u = chunks + e
        wait(hidden.at[1, e], y_recv.at[0, u])
        send(hidden.at[1, e, low], hidden.at[3, e, low], y_send.at[2, u], y_recv.at[2, u], y_peer(right))
        wait(hidden.at[2, e], y_recv.at[1, u])
        send(hidden.at[2, e, high], hidden.at[3, e, high], y_send.at[3, u], y_recv.at[3, u], y_peer(left))
    load_d.wait()
    for slot in (1, 2, 3):
        wait(wd.at[slot], wd_recv.at[slot - 1])
    for e in range(2):
        u = chunks + e
        wait(hidden.at[3, e, low], y_recv.at[2, u])
        wait(hidden.at[3, e, high], y_recv.at[3, u])

    def stage_e(k):
        cols = pl.ds(pl.multiple_of(k * LANES, LANES), LANES)
        for e in range(2):
            total = jnp.zeros((nd * grp, LANES), f32)
            for s in range(NY):
                total = total + jnp.dot(hidden[s, e], wd[s, e, :, cols], preferred_element_type=f32)
            value = total.astype(bf16).reshape(nd, grp, LANES)
            outs[k, :, e] = value
            back[k, 0, e] = value[0]

        def one(r, carry):
            send(outs.at[k, r], back.at[k, r], b_send.at[k], b_recv.at[k], d_peer(nd - r))
            return carry

        lax.fori_loop(1, nd, one, 0)

    def stage_f(k):
        wait(back.at[k, pl.ds(1, nd - 1)], b_recv.at[k])
        per = nz // 2
        for i in range(2):
            value = jnp.dot(
                cmb[i * per * tok:(i + 1) * per * tok, :],
                back[k].reshape(2 * nd * grp, LANES),
                preferred_element_type=f32,
            ).astype(bf16).reshape(per, tok, LANES)
            part[k, i * per:(i + 1) * per] = value
            for j in range(max(1, i * per), (i + 1) * per):
                send(part.at[k, j], home.at[k, j], h_send.at[k], h_recv.at[k], z_peer(nz - j))

    def stage_g(k):
        @pl.when(k == 0)
        def _():
            for slot in (1, 2, 3):
                wait(pieces_y.at[slot - 1], p_recv.at[slot - 1])

        cols = pl.ds(pl.multiple_of(k * LANES, LANES), LANES)
        wait(home.at[k, pl.ds(1, nz - 1)], h_recv.at[k])
        total = part[k, 0].astype(f32) + pieces[0, :, cols].astype(f32)
        for slot in (1, 2, 3):
            total = total + pieces_y[slot - 1, :, cols].astype(f32)
        for j in range(1, nz):
            total = total + home[k, j].astype(f32)
        out_ref[:, cols] = total.astype(bf16)

    lag_f, lag_g = 1, 3

    def step_back(i, carry):
        @pl.when(i < chunks)
        def _():
            stage_e(i)

        @pl.when((i >= lag_f) & (i < chunks + lag_f))
        def _():
            stage_f(i - lag_f)

        @pl.when(i >= lag_g)
        def _():
            stage_g(i - lag_g)

        return carry

    lax.fori_loop(0, chunks + lag_g, step_back, 0)

    wait(meta.at[:, :, pl.ds(tok, (nz - 1) * tok)], meta_send)
    wait(shards.at[:, pl.ds(1, nz - 1), d], sz_send)
    for r in range(nx):
        if r:
            wait(shards.at[:, :, d], sx_send.at[r - 1])
        wait(shards.at[:, :, d_of(r, core)], sc_send.at[r])
    for slot in (1, 2, 3):
        wait(tokens_y.at[slot - 1], t_send.at[slot - 1])
        wait(pieces.at[slot], p_send.at[slot - 1])
        wait(wd.at[slot], wd_send.at[slot - 1])

    def drain(k, carry):
        wait(held.at[k, pl.ds(1, nz - 1)], z_send.at[k])
        wait(packed.at[k, pl.ds(1, nd - 1)], x_send.at[k])
        wait(rows.at[0, k], y_send.at[0, k])
        wait(rows.at[0, k], y_send.at[1, k])
        wait(rows.at[1, k, 0], y_send.at[2, k])
        wait(rows.at[2, k, 1], y_send.at[3, k])
        wait(outs.at[k, pl.ds(1, nd - 1)], b_send.at[k])
        wait(part.at[k, pl.ds(1, nz - 1)], h_send.at[k])
        return carry

    lax.fori_loop(0, chunks, drain, 0)
    for e in range(2):
        u = chunks + e
        wait(hidden.at[0, e], y_send.at[0, u])
        wait(hidden.at[0, e], y_send.at[1, u])
        wait(hidden.at[1, e, low], y_send.at[2, u])
        wait(hidden.at[2, e, high], y_send.at[3, u])


def layer(tokens, expert_ids, gate_weights, w_gate, w_up, w_down, shard, cap):
    nz, nx = dims_of(lax.axis_size("exp"))
    nd = nx * NC
    tok, quarter = tokens.shape
    top = expert_ids.shape[1]
    width, hid = w_gate.shape[1:]
    chunks = quarter // LANES
    grp = nz * cap
    f32, bf16 = jnp.float32, jnp.bfloat16
    dma = pltpu.SemaphoreType.DMA
    vm = pltpu.VMEM
    slots = 2 * nd * grp
    rp = shard.shape[1]
    padded_cols = quarter // (width // (nz * nd)) * rp
    hbm = pl.BlockSpec(memory_space=pl.ANY)
    inside = pl.BlockSpec(memory_space=pltpu.VMEM)
    return pl.pallas_call(
        functools.partial(layer_kernel, nz, nd, cap, tok, top, chunks, hid),
        out_shape=jax.ShapeDtypeStruct((tok, quarter), bf16),
        in_specs=[inside, inside, inside, hbm, hbm, hbm, inside],
        out_specs=inside,
        scratch_shapes=[
            vm((2, width, hid), bf16),
            vm((2, width, hid), bf16),
            vm((NY, 2, hid, quarter), bf16),
            vm((2, 2 * nz * nd, tok), f32),
            vm((2, 2 * nd, nz * tok), f32),
            vm((2 * nd, grp, nz * tok), bf16),
            vm((slots, nz * tok), bf16),
            vm((nz * tok, slots), bf16),
            vm((chunks, nz, tok, LANES), bf16),
            vm((chunks, nd, 2, grp, LANES), bf16),
            vm((NY, chunks, 2, nd, grp, LANES), bf16),
            vm((2, 2, nd // 2 * grp, hid), f32),
            vm((2, 2, nd // 2 * grp, hid), f32),
            vm((NY, 2, nd * grp, hid), bf16),
            vm((chunks, nd, 2, grp, LANES), bf16),
            vm((chunks, nd, 2, grp, LANES), bf16),
            vm((chunks, nz, tok, LANES), bf16),
            vm((chunks, nz, tok, LANES), bf16),
            vm((quarter, padded_cols), bf16),
            vm((3, nz, nd, rp, hid), bf16),
            vm((NY - 1, tok, quarter), bf16),
            vm((tok, padded_cols), bf16),
            vm((NY, tok, quarter), bf16),
            vm((NY - 1, tok, quarter), bf16),
            dma((3,)), dma((3,)), dma((3,)), dma, dma,
            dma((chunks,)), dma((chunks,)), dma((chunks,)), dma((chunks,)),
            dma((4, chunks + 2)), dma((4, chunks + 2)),
            dma((chunks,)), dma((chunks,)), dma((chunks,)), dma((chunks,)),
            dma, dma, dma((max(1, nx - 1),)), dma((max(1, nx - 1),)), dma((nx,)), dma((nx,)),
            dma((3,)), dma((3,)), dma((3,)), dma((3,)),
        ],
        compiler_params=pltpu.CompilerParams(
            collective_id=0, has_side_effects=True, vmem_limit_bytes=60 * 1024 * 1024
        ),
        cost_estimate=pl.CostEstimate(
            flops=2 * slots * width * hid * 3, bytes_accessed=6 * width * hid * 2, transcendentals=slots * hid
        ),
        name="layer",
    )(tokens, expert_ids, gate_weights, w_gate, w_up, w_down, shard)


def body(tokens, expert_ids, gate_weights, w_gate, w_up, w_down, s_gate, s_up, s_down):
    exp_count = lax.axis_size("exp")
    tok_count, top_count = expert_ids.shape
    experts = w_gate.shape[0] * exp_count
    capacity = max(2, 5 * tok_count * top_count // (4 * experts))
    rows = s_gate.shape[0]
    shard = jnp.stack([s_gate, s_up, s_down.T])
    shard = jnp.pad(shard, ((0, 0), (0, -rows % 64), (0, 0)))
    return layer(tokens, expert_ids, gate_weights, w_gate, w_up, w_down, shard, capacity)


def solution(mesh):
    return jax.shard_map(
        body,
        mesh=mesh,
        in_specs=(
            P("exp", "tp"),
            P("exp", None),
            P("exp", None),
            P("exp", None, "tp"),
            P("exp", None, "tp"),
            P("exp", "tp", None),
            P("exp", "tp"),
            P("exp", "tp"),
            P("tp", "exp"),
        ),
        out_specs=P("exp", "tp"),
        check_vma=False,
    )
```

```python
import functools

import jax
import jax.numpy as jnp
from jax import lax
from jax.experimental import pallas as pl
from jax.experimental.pallas import tpu as pltpu
from jax.sharding import PartitionSpec as P

MESH = pl.DeviceIdType.MESH
NY = 4
NC = 2
LANES = 128


def dims_of(exp_count):
    nz, nx = {64: (8, 4), 4: (2, 1)}[exp_count]
    return nz, nx


def layer_kernel(
    nz, nd, cap, tok, top, chunks, hid,
    tokens_ref, ids_ref, wts_ref, wg_hbm, wu_hbm, wd_hbm, shard_ref,
    out_ref,
    wg, wu, wd, score, meta, sel, cmb, order, held, packed, rows, gate, upper, hidden,
    outs, back, part, home, turned,
    spread, shards, tokens_y, padded, pieces, pieces_y,
    load_sem, wd_send, wd_recv, meta_send, meta_recv, z_send, z_recv, x_send, x_recv,
    y_send, y_recv, b_send, b_recv, h_send, h_recv,
    sz_send, sz_recv, sx_send, sx_recv, sc_send, sc_recv, t_send, t_recv, p_send, p_recv,
):
    quarter = chunks * LANES
    grp = nz * cap
    f32, bf16 = jnp.float32, jnp.bfloat16
    exp = lax.axis_index("exp")
    y = lax.axis_index("tp")
    z = exp // nd
    d = exp % nd
    right = (y + 1) % NY
    left = (y + NY - 1) % NY
    across = (y + 2) % NY

    def z_peer(j):
        return (((z + j) % nz) * nd + d, y)

    def d_peer(r):
        return (z * nd + (d + r) % nd, y)

    def y_peer(q):
        return (exp, q)

    nx = nd // NC
    x = d // NC
    core = d % NC

    def d_of(r, c):
        return ((x + nx - r) % nx) * NC + c

    def send(src, dst, ss, rs, dev):
        pltpu.make_async_remote_copy(
            src_ref=src, dst_ref=dst, send_sem=ss, recv_sem=rs, device_id=dev, device_id_type=MESH
        ).start()

    def wait(ref, sem):
        pltpu.make_async_copy(ref, ref, sem).wait()

    load_g = pltpu.make_async_copy(wg_hbm, wg, load_sem.at[0])
    load_u = pltpu.make_async_copy(wu_hbm, wu, load_sem.at[1])
    load_d = pltpu.make_async_copy(wd_hbm.at[:, :, pl.ds(y * quarter, quarter)], wd.at[0], load_sem.at[2])
    load_g.start()
    load_u.start()
    load_d.start()

    barrier = pltpu.get_barrier_semaphore()
    for j in range(1, nz):
        pl.semaphore_signal(barrier, inc=1, device_id=z_peer(j), device_id_type=MESH)
    for r in range(1, nd):
        pl.semaphore_signal(barrier, inc=1, device_id=d_peer(r), device_id_type=MESH)
    for q in (left, right, across):
        pl.semaphore_signal(barrier, inc=1, device_id=y_peer(q), device_id_type=MESH)

    experts = nz * nd * 2
    names = lax.broadcasted_iota(jnp.int32, (experts, tok), 0)
    named = jnp.zeros((experts, tok), f32)
    weight = jnp.zeros((experts, tok), f32)
    for k in range(top):
        hit = ids_ref[k:k + 1, :] == names
        named = named + jnp.where(hit, 1.0, 0.0)
        weight = weight + jnp.where(hit, wts_ref[k:k + 1, :], 0.0)
    before = lax.broadcasted_iota(jnp.int32, (tok, tok), 0) < lax.broadcasted_iota(jnp.int32, (tok, tok), 1)
    rank = jnp.dot(
        named.astype(bf16), jnp.where(before, 1.0, 0.0).astype(bf16), preferred_element_type=f32
    )
    score[0] = jnp.where(named > 0.5, rank, -1.0)
    score[1] = weight
    plane = 2 * nd

    pl.semaphore_wait(barrier, nz - 1 + nd - 1 + 3)

    for j in range(1, nz):
        zj = (z + j) % nz
        send(
            score.at[0, pl.ds(pl.multiple_of(zj * plane, plane), plane), :],
            meta.at[:, pl.ds(j * tok, tok)],
            meta_send, meta_recv, z_peer(j),
        )
    meta[:, 0:tok] = score[0, pl.ds(pl.multiple_of(z * plane, plane), plane), :]

    y_slots = ((1, right), (2, left), (3, across))
    for slot, q in y_slots:
        send(tokens_ref, tokens_y.at[slot - 1], t_send.at[slot - 1], t_recv.at[slot - 1], y_peer(q))

    def send_tokens(k, carry):
        cols = pl.ds(pl.multiple_of(k * LANES, LANES), LANES)
        for j in range(1, nz):
            send(tokens_ref.at[:, cols], held.at[k, j], z_send.at[k], z_recv.at[k], z_peer(j))
        held[k, 0] = tokens_ref[:, cols]
        return carry

    lax.fori_loop(0, chunks, send_tokens, 0)

    for j in range(1, nz):
        send(shard_ref, shards.at[:, j, d], sz_send, sz_recv, z_peer(j))
    shards[:, 0, d] = shard_ref[...]

    for slot, q in y_slots:
        send(
            wd_hbm.at[:, :, pl.ds(pl.multiple_of(q * quarter, LANES), quarter)],
            wd.at[slot], wd_send.at[slot - 1], wd_recv.at[slot - 1], y_peer(q),
        )

    wait(meta.at[:, pl.ds(tok, (nz - 1) * tok)], meta_recv)

    row = lax.broadcasted_iota(jnp.int32, (grp, nz * tok), 0)
    col = lax.broadcasted_iota(jnp.int32, (grp, nz * tok), 1)
    wanted = jnp.where(row % nz == col // tok, row // nz, -5).astype(f32)

    def build(g, carry):
        index = ((d + g % nd) % nd) * 2 + g // nd
        hit = meta[pl.ds(index, 1), :] == wanted
        sel[g // nd, g % nd] = jnp.where(hit, 1.0, 0.0).astype(bf16)
        return carry

    lax.fori_loop(0, 2 * nd, build, 0)

    gate[...] = jnp.zeros_like(gate)
    upper[...] = jnp.zeros_like(upper)
    slots = nd * grp

    def stage_a(u):
        e = u // chunks
        k = u % chunks

        @pl.when(e == 0)
        def _():
            wait(held.at[k, pl.ds(1, nz - 1)], z_recv.at[k])

        packed[u] = jnp.dot(
            sel[e].reshape(slots, nz * tok), held[k].reshape(nz * tok, LANES), preferred_element_type=f32
        ).astype(bf16).reshape(nd, grp, LANES)
        for r in range(1, nd):
            send(packed.at[u, r], rows.at[0, u, r], x_send.at[u], x_recv.at[u], d_peer(r))
        rows[0, u, 0] = packed[u, 0]

    def stage_b(u):
        wait(rows.at[0, u, pl.ds(1, nd - 1)], x_recv.at[u])
        send(rows.at[0, u], rows.at[1, u], y_send.at[0, u], y_recv.at[0, u], y_peer(right))
        send(rows.at[0, u], rows.at[2, u], y_send.at[1, u], y_recv.at[1, u], y_peer(left))

    halves = nd // 2
    first, second = pl.ds(0, halves), pl.ds(halves, halves)

    def accumulate(u, sources):
        e = u // chunks
        k = u % chunks

        def one(h, carry):
            g = gate[e, h]
            up = upper[e, h]
            for s, q in sources:
                x = rows[s, u, pl.ds(h * halves, halves)].reshape(halves * grp, LANES)
                at = pl.ds(pl.multiple_of(q * quarter + k * LANES, LANES), LANES)
                g = g + jnp.dot(x, wg[e, at, :], preferred_element_type=f32)
                up = up + jnp.dot(x, wu[e, at, :], preferred_element_type=f32)
            gate[e, h] = g
            upper[e, h] = up
            return carry

        lax.fori_loop(0, 2, one, 0)

    def stage_c(u):
        wait(rows.at[1, u], y_recv.at[0, u])
        send(rows.at[1, u, first], rows.at[3, u, first], y_send.at[2, u], y_recv.at[2, u], y_peer(right))
        wait(rows.at[2, u], y_recv.at[1, u])
        send(rows.at[2, u, second], rows.at[3, u, second], y_send.at[3, u], y_recv.at[3, u], y_peer(left))
        accumulate(u, ((0, y), (1, left), (2, right)))

    def stage_d(u):
        wait(rows.at[3, u, first], y_recv.at[2, u])
        wait(rows.at[3, u, second], y_recv.at[3, u])
        accumulate(u, ((3, across),))

    half_rows = halves * grp
    low, high = pl.ds(0, half_rows), pl.ds(half_rows, half_rows)
    units = 2 * chunks

    def hidden_out(e):
        for h in range(2):
            g = gate[e, h]
            hidden[0, e, h * half_rows:(h + 1) * half_rows, :] = (
                g / (1.0 + jnp.exp(-g)) * upper[e, h]
            ).astype(bf16)
        u = units + e
        send(hidden.at[0, e], hidden.at[1, e], y_send.at[0, u], y_recv.at[0, u], y_peer(right))
        send(hidden.at[0, e], hidden.at[2, e], y_send.at[1, u], y_recv.at[1, u], y_peer(left))

    def hidden_on(e):
        u = units + e
        wait(hidden.at[1, e], y_recv.at[0, u])
        send(hidden.at[1, e, low], hidden.at[3, e, low], y_send.at[2, u], y_recv.at[2, u], y_peer(right))
        wait(hidden.at[2, e], y_recv.at[1, u])
        send(hidden.at[2, e, high], hidden.at[3, e, high], y_send.at[3, u], y_recv.at[3, u], y_peer(left))

    def hidden_in(e):
        u = units + e
        wait(hidden.at[3, e, low], y_recv.at[2, u])
        wait(hidden.at[3, e, high], y_recv.at[3, u])

    def stage_e(e, k):
        cols = pl.ds(pl.multiple_of(k * LANES, LANES), LANES)
        total = jnp.zeros((slots, LANES), f32)
        for s in range(NY):
            total = total + jnp.dot(hidden[s, e], wd[s, e, :, cols], preferred_element_type=f32)
        value = total.astype(bf16).reshape(nd, grp, LANES)
        outs[e, k] = value
        back[e, k, 0] = value[0]
        for r in range(1, nd):
            send(outs.at[e, k, r], back.at[e, k, r], b_send.at[e, k], b_recv.at[e, k], d_peer(nd - r))

    def stage_f(e, k):
        wait(back.at[e, k, pl.ds(1, nd - 1)], b_recv.at[e, k])
        value = jnp.dot(
            order[...], back[e, k].reshape(slots, LANES), preferred_element_type=f32
        ).astype(bf16).reshape(nz, nd * cap, LANES)
        part[e, k] = value
        home[e, k, 0] = value[0]
        for j in range(1, nz):
            send(part.at[e, k, j], home.at[e, k, j], h_send.at[e, k], h_recv.at[e, k], z_peer(nz - j))

    def stage_g(k):
        @pl.when(k == 0)
        def _():
            for slot in (1, 2, 3):
                wait(pieces_y.at[slot - 1], p_recv.at[slot - 1])

        cols = pl.ds(pl.multiple_of(k * LANES, LANES), LANES)
        total = pieces[0, :, cols].astype(f32)
        for slot in (1, 2, 3):
            total = total + pieces_y[slot - 1, :, cols].astype(f32)
        for e in range(2):
            wait(home.at[e, k, pl.ds(1, nz - 1)], h_recv.at[e, k])
            total = total + jnp.dot(
                cmb[e], home[e, k].reshape(nz * nd * cap, LANES), preferred_element_type=f32
            )
        out_ref[:, cols] = total.astype(bf16)

    def build_return():
        at = lax.broadcasted_iota(jnp.int32, (slots, slots), 0)
        lane = lax.broadcasted_iota(jnp.int32, (1, slots), 1)
        source = lane % grp
        target = (source % nz) * (nd * cap) + source // nz * nd + (d + lane // grp) % nd
        order[...] = jnp.where(at == target, 1.0, 0.0).astype(bf16)

        for e in range(2):
            for j in range(nz):
                base = ((z + j) % nz) * plane + e
                ranks = score[0, pl.ds(base, nd, 2), :]
                weights = score[1, pl.ds(base, nd, 2), :]
                for p in range(cap):
                    at_row = (j * cap + p) * nd
                    turned[at_row:at_row + nd, :] = jnp.where(ranks == p, weights, 0.0)
            for a in range(nz * nd * cap // LANES):
                block = slice(a * LANES, (a + 1) * LANES)
                cmb[e, :, block] = turned[block, :].T.astype(bf16)

    def shards_in_plane():
        wait(shards.at[:, pl.ds(1, nz - 1), d], sz_recv)
        mine = shards.at[:, :, d]
        for r in range(1, nx):
            send(mine, mine, sx_send.at[r - 1], sx_recv.at[r - 1], (z * nd + ((x + r) % nx) * NC + core, y))
        send(mine, mine, sc_send.at[0], sc_recv.at[0], (z * nd + x * NC + 1 - core, y))

    def shards_in_chip():
        for r in range(1, nx):
            block = shards.at[:, :, d_of(r, core)]
            wait(block, sx_recv.at[r - 1])
            send(block, block, sc_send.at[r], sc_recv.at[r], (z * nd + x * NC + 1 - core, y))

    rp = shard_ref.shape[1]
    rs = quarter * NY // (nz * nd)
    per_quarter = quarter // rs
    run = min(per_quarter, nd)

    def spread_matrix():
        into = lax.broadcasted_iota(jnp.int32, spread.shape, 1)
        at = lax.broadcasted_iota(jnp.int32, spread.shape, 0)
        inner = into % rp
        spread[...] = jnp.where((inner < rs) & (at == into // rp * rs + inner), 1.0, 0.0).astype(bf16)

    def block_of(m, q, i):
        first = q * per_quarter + i * run
        zr = (z + nz - first // nd) % nz
        return shards[m, zr, pl.ds(first % nd, run)].reshape(run * rp, hid)

    def shared_expert():
        for r in range(nx):
            wait(shards.at[:, :, d_of(r, 1 - core)], sc_recv.at[r])
        s_gate = jnp.zeros((tok, hid), f32)
        s_upper = jnp.zeros((tok, hid), f32)
        for slot, q in ((0, y), (1, left), (2, right), (3, across)):
            if slot:
                wait(tokens_y.at[slot - 1], t_recv.at[slot - 1])
            source = tokens_y[slot - 1] if slot else tokens_ref[...]
            padded[...] = jnp.dot(source, spread[...], preferred_element_type=f32).astype(bf16)
            for i in range(per_quarter // run):
                lhs = padded[:, i * run * rp:(i + 1) * run * rp]
                s_gate = s_gate + jnp.dot(lhs, block_of(0, q, i), preferred_element_type=f32)
                s_upper = s_upper + jnp.dot(lhs, block_of(1, q, i), preferred_element_type=f32)
        act = (s_gate / (1.0 + jnp.exp(-s_gate)) * s_upper).astype(bf16)
        across_rows = (((1,), (1,)), ((), ()))
        for slot, q in ((1, right), (2, left), (3, across), (0, y)):
            for i in range(per_quarter // run):
                padded[:, i * run * rp:(i + 1) * run * rp] = lax.dot_general(
                    act, block_of(2, q, i), across_rows, preferred_element_type=f32
                ).astype(bf16)
            pieces[slot] = lax.dot_general(
                padded[...], spread[...], across_rows, preferred_element_type=f32
            ).astype(bf16)
            if slot:
                send(pieces.at[slot], pieces_y.at[slot - 1], p_send.at[slot - 1], p_recv.at[slot - 1], y_peer(q))

    load_g.wait()
    load_u.wait()

    lag_b, lag_c, lag_d = 1, 2, 4

    def at_step(i, n, *calls):
        @pl.when(i == n)
        def _():
            for call in calls:
                call()

    def all_chunks(stage, e):
        def one(k, carry):
            stage(e, k)
            return carry

        lax.fori_loop(0, chunks, one, 0)

    def finish_first():
        load_d.wait()
        for slot in (1, 2, 3):
            wait(wd.at[slot], wd_recv.at[slot - 1])
        hidden_in(0)
        all_chunks(stage_e, 0)

    ready = chunks - 1 + lag_d

    def step(i, carry):
        @pl.when(i < units)
        def _():
            stage_a(i)

        @pl.when((i >= lag_b) & (i < units + lag_b))
        def _():
            stage_b(i - lag_b)

        at_step(i, 2, build_return)
        at_step(i, 4, spread_matrix)
        at_step(i, 5, shards_in_plane)
        at_step(i, 9, shards_in_chip)

        @pl.when((i >= lag_c) & (i < units + lag_c))
        def _():
            stage_c(i - lag_c)

        @pl.when(i >= lag_d)
        def _():
            stage_d(i - lag_d)

        at_step(i, ready, lambda: hidden_out(0))
        at_step(i, ready + 1, lambda: hidden_on(0))
        at_step(i, ready + 2, finish_first)
        at_step(i, ready + 3, shared_expert)
        at_step(i, ready + 4, lambda: all_chunks(stage_f, 0))
        return carry

    lax.fori_loop(0, units + lag_d, step, 0)

    hidden_out(1)
    hidden_on(1)
    hidden_in(1)

    lag_f, lag_g = 1, 3

    def step_back(i, carry):
        @pl.when(i < chunks)
        def _():
            stage_e(1, i)

        @pl.when((i >= lag_f) & (i < chunks + lag_f))
        def _():
            stage_f(1, i - lag_f)

        @pl.when(i >= lag_g)
        def _():
            stage_g(i - lag_g)

        return carry

    lax.fori_loop(0, chunks + lag_g, step_back, 0)

    wait(meta.at[:, pl.ds(tok, (nz - 1) * tok)], meta_send)
    wait(shards.at[:, pl.ds(1, nz - 1), d], sz_send)
    for r in range(nx):
        if r:
            wait(shards.at[:, :, d], sx_send.at[r - 1])
        wait(shards.at[:, :, d_of(r, core)], sc_send.at[r])
    for slot in (1, 2, 3):
        wait(tokens_y.at[slot - 1], t_send.at[slot - 1])
        wait(pieces.at[slot], p_send.at[slot - 1])
        wait(wd.at[slot], wd_send.at[slot - 1])

    def drain(k, carry):
        wait(held.at[k, pl.ds(1, nz - 1)], z_send.at[k])
        for e in range(2):
            wait(outs.at[e, k, pl.ds(1, nd - 1)], b_send.at[e, k])
            wait(part.at[e, k, pl.ds(1, nz - 1)], h_send.at[e, k])
        return carry

    lax.fori_loop(0, chunks, drain, 0)

    def drain_units(u, carry):
        wait(packed.at[u, pl.ds(1, nd - 1)], x_send.at[u])
        wait(rows.at[0, u], y_send.at[0, u])
        wait(rows.at[0, u], y_send.at[1, u])
        wait(rows.at[1, u, first], y_send.at[2, u])
        wait(rows.at[2, u, second], y_send.at[3, u])
        return carry

    lax.fori_loop(0, units, drain_units, 0)
    for e in range(2):
        u = units + e
        wait(hidden.at[0, e], y_send.at[0, u])
        wait(hidden.at[0, e], y_send.at[1, u])
        wait(hidden.at[1, e, low], y_send.at[2, u])
        wait(hidden.at[2, e, high], y_send.at[3, u])


def layer(tokens, expert_ids, gate_weights, w_gate, w_up, w_down, shard, cap):
    nz, nx = dims_of(lax.axis_size("exp"))
    nd = nx * NC
    tok, quarter = tokens.shape
    top = expert_ids.shape[1]
    width, hid = w_gate.shape[1:]
    chunks = quarter // LANES
    grp = nz * cap
    f32, bf16 = jnp.float32, jnp.bfloat16
    dma = pltpu.SemaphoreType.DMA
    vm = pltpu.VMEM
    slots = 2 * nd * grp
    rp = shard.shape[1]
    padded_cols = quarter // (width // (nz * nd)) * rp
    hbm = pl.BlockSpec(memory_space=pl.ANY)
    inside = pl.BlockSpec(memory_space=pltpu.VMEM)
    return pl.pallas_call(
        functools.partial(layer_kernel, nz, nd, cap, tok, top, chunks, hid),
        out_shape=jax.ShapeDtypeStruct((tok, quarter), bf16),
        in_specs=[inside, inside, inside, hbm, hbm, hbm, inside],
        out_specs=inside,
        scratch_shapes=[
            vm((2, width, hid), bf16),
            vm((2, width, hid), bf16),
            vm((NY, 2, hid, quarter), bf16),
            vm((2, 2 * nz * nd, tok), f32),
            vm((2 * nd, nz * tok), f32),
            vm((2, nd, grp, nz * tok), bf16),
            vm((2, tok, nz * nd * cap), bf16),
            vm((nd * grp, nd * grp), bf16),
            vm((chunks, nz, tok, LANES), bf16),
            vm((2 * chunks, nd, grp, LANES), bf16),
            vm((NY, 2 * chunks, nd, grp, LANES), bf16),
            vm((2, 2, nd // 2 * grp, hid), f32),
            vm((2, 2, nd // 2 * grp, hid), f32),
            vm((NY, 2, nd * grp, hid), bf16),
            vm((2, chunks, nd, grp, LANES), bf16),
            vm((2, chunks, nd, grp, LANES), bf16),
            vm((2, chunks, nz, nd * cap, LANES), bf16),
            vm((2, chunks, nz, nd * cap, LANES), bf16),
            vm((nz * nd * cap, tok), f32),
            vm((quarter, padded_cols), bf16),
            vm((3, nz, nd, rp, hid), bf16),
            vm((NY - 1, tok, quarter), bf16),
            vm((tok, padded_cols), bf16),
            vm((NY, tok, quarter), bf16),
            vm((NY - 1, tok, quarter), bf16),
            dma((3,)), dma((3,)), dma((3,)), dma, dma,
            dma((chunks,)), dma((chunks,)), dma((2 * chunks,)), dma((2 * chunks,)),
            dma((4, 2 * chunks + 2)), dma((4, 2 * chunks + 2)),
            dma((2, chunks)), dma((2, chunks)), dma((2, chunks)), dma((2, chunks)),
            dma, dma, dma((max(1, nx - 1),)), dma((max(1, nx - 1),)), dma((nx,)), dma((nx,)),
            dma((3,)), dma((3,)), dma((3,)), dma((3,)),
        ],
        compiler_params=pltpu.CompilerParams(
            collective_id=0, has_side_effects=True, vmem_limit_bytes=60 * 1024 * 1024
        ),
        cost_estimate=pl.CostEstimate(
            flops=2 * slots * width * hid * 3, bytes_accessed=6 * width * hid * 2, transcendentals=slots * hid
        ),
        name="layer",
    )(tokens, expert_ids.T, gate_weights.T, w_gate, w_up, w_down, shard)


def body(tokens, expert_ids, gate_weights, w_gate, w_up, w_down, s_gate, s_up, s_down):
    exp_count = lax.axis_size("exp")
    tok_count, top_count = expert_ids.shape
    experts = w_gate.shape[0] * exp_count
    capacity = max(2, 5 * tok_count * top_count // (4 * experts))
    rows = s_gate.shape[0]
    shard = jnp.stack([s_gate, s_up, s_down.T])
    shard = jnp.pad(shard, ((0, 0), (0, -rows % 64), (0, 0)))
    return layer(tokens, expert_ids, gate_weights, w_gate, w_up, w_down, shard, capacity)


def solution(mesh):
    return jax.shard_map(
        body,
        mesh=mesh,
        in_specs=(
            P("exp", "tp"),
            P("exp", None),
            P("exp", None),
            P("exp", None, "tp"),
            P("exp", None, "tp"),
            P("exp", "tp", None),
            P("exp", "tp"),
            P("exp", "tp"),
            P("tp", "exp"),
        ),
        out_specs=P("exp", "tp"),
        check_vma=False,
    )
```

```python
import functools

import jax
import jax.numpy as jnp
from jax import lax
from jax.experimental import pallas as pl
from jax.experimental.pallas import tpu as pltpu
from jax.sharding import PartitionSpec as P

MESH = pl.DeviceIdType.MESH
NY = 4
NC = 2
LANES = 128
EARLY = 0


def dims_of(exp_count):
    nz, nx = {64: (8, 4), 4: (2, 1)}[exp_count]
    return nz, nx


def layer_kernel(
    nz, nd, cap, tok, top, chunks, hid,
    tokens_ref, ids_ref, wts_ref, wg_hbm, wu_hbm, wd_hbm, shard_ref,
    out_ref,
    wg, wu, wd, score, meta, sel, cmb, order, held, packed, rows, gate, upper, hidden,
    outs, back, part, home, turned,
    spread, shards, tokens_y, padded, pieces, pieces_y,
    load_sem, wd_send, wd_recv, meta_send, meta_recv, z_send, z_recv, x_send, x_recv,
    y_send, y_recv, b_send, b_recv, h_send, h_recv,
    sz_send, sz_recv, sx_send, sx_recv, sc_send, sc_recv, t_send, t_recv, p_send, p_recv,
):
    quarter = chunks * LANES
    z_ahead = 3
    early = min(EARLY, chunks - 3)
    late = chunks - early
    parts = late + NY * early
    grp = nz * cap
    f32, bf16 = jnp.float32, jnp.bfloat16
    exp = lax.axis_index("exp")
    y = lax.axis_index("tp")
    z = exp // nd
    d = exp % nd
    right = (y + 1) % NY
    left = (y + NY - 1) % NY
    across = (y + 2) % NY

    def z_peer(j):
        return (((z + j) % nz) * nd + d, y)

    def d_peer(r):
        return (z * nd + (d + r) % nd, y)

    def y_peer(q):
        return (exp, q)

    nx = nd // NC
    x = d // NC
    core = d % NC

    def d_of(r, c):
        return ((x + nx - r) % nx) * NC + c

    def send(src, dst, ss, rs, dev):
        pltpu.make_async_remote_copy(
            src_ref=src, dst_ref=dst, send_sem=ss, recv_sem=rs, device_id=dev, device_id_type=MESH
        ).start()

    def wait(ref, sem):
        pltpu.make_async_copy(ref, ref, sem).wait()

    load_g = pltpu.make_async_copy(wg_hbm, wg, load_sem.at[0])
    load_u = pltpu.make_async_copy(wu_hbm, wu, load_sem.at[1])
    load_d = pltpu.make_async_copy(wd_hbm.at[:, :, pl.ds(y * quarter, quarter)], wd.at[0], load_sem.at[2])
    load_g.start()
    load_u.start()
    load_d.start()

    barrier = pltpu.get_barrier_semaphore()
    for j in range(1, nz):
        pl.semaphore_signal(barrier, inc=1, device_id=z_peer(j), device_id_type=MESH)
    for r in range(1, nd):
        pl.semaphore_signal(barrier, inc=1, device_id=d_peer(r), device_id_type=MESH)
    for q in (left, right, across):
        pl.semaphore_signal(barrier, inc=1, device_id=y_peer(q), device_id_type=MESH)

    experts = nz * nd * 2
    names = lax.broadcasted_iota(jnp.int32, (experts, tok), 0)
    named = jnp.zeros((experts, tok), f32)
    weight = jnp.zeros((experts, tok), f32)
    for k in range(top):
        hit = ids_ref[k:k + 1, :] == names
        named = named + jnp.where(hit, 1.0, 0.0)
        weight = weight + jnp.where(hit, wts_ref[k:k + 1, :], 0.0)
    before = lax.broadcasted_iota(jnp.int32, (tok, tok), 0) < lax.broadcasted_iota(jnp.int32, (tok, tok), 1)
    rank = jnp.dot(
        named.astype(bf16), jnp.where(before, 1.0, 0.0).astype(bf16), preferred_element_type=f32
    )
    score[0] = jnp.where(named > 0.5, rank, -1.0)
    score[1] = weight
    plane = 2 * nd

    pl.semaphore_wait(barrier, nz - 1 + nd - 1 + 3)

    for j in range(1, nz):
        zj = (z + j) % nz
        send(
            score.at[0, pl.ds(pl.multiple_of(zj * plane, plane), plane), :],
            meta.at[:, pl.ds(j * tok, tok)],
            meta_send, meta_recv, z_peer(j),
        )
    meta[:, 0:tok] = score[0, pl.ds(pl.multiple_of(z * plane, plane), plane), :]

    y_slots = ((1, right), (2, left), (3, across))

    def send_tokens(i, source, k):
        cols = pl.ds(pl.multiple_of(k * LANES, LANES), LANES)
        for j in range(1, nz):
            send(source.at[:, cols], held.at[i, j], z_send.at[i], z_recv.at[i], z_peer(j))
        held[i, 0] = source[:, cols]

    def send_late(k):
        send_tokens(k, tokens_ref, k)

    def send_early(n):
        if n == 0:
            for slot in (1, 2, 3):
                wait(tokens_y.at[slot - 1], t_recv.at[slot - 1])
        for slot in range(NY):
            source = tokens_y.at[slot - 1] if slot else tokens_ref
            send_tokens(late + NY * n + slot, source, late + n)

    def send_tokens_y():
        for slot, q in y_slots:
            send(tokens_ref, tokens_y.at[slot - 1], t_send.at[slot - 1], t_recv.at[slot - 1], y_peer(q))

    def send_wd(u):
        e = u // chunks
        k = u % chunks
        for slot, q in y_slots:
            send(
                wd_hbm.at[e, :, pl.ds(pl.multiple_of(q * quarter + k * LANES, LANES), LANES)],
                wd.at[slot, e, :, pl.ds(pl.multiple_of(k * LANES, LANES), LANES)],
                wd_send.at[slot - 1, e], wd_recv.at[slot - 1, e], y_peer(q),
            )

    def send_shard():
        for j in range(1, nz):
            send(shard_ref, shards.at[:, j, d], sz_send, sz_recv, z_peer(j))
        shards[:, 0, d] = shard_ref[...]

    send_late(0)
    send_tokens_y()
    for k in range(1, z_ahead):
        send_late(k)
    wd_first = min(4, 2 * chunks - 2 * late)
    for u in range(wd_first):
        send_wd(u)

    wait(meta.at[:, pl.ds(tok, (nz - 1) * tok)], meta_recv)

    row = lax.broadcasted_iota(jnp.int32, (grp, nz * tok), 0)
    col = lax.broadcasted_iota(jnp.int32, (grp, nz * tok), 1)
    wanted = jnp.where(row % nz == col // tok, row // nz, -5).astype(f32)

    def build(g, carry):
        index = ((d + g % nd) % nd) * 2 + g // nd
        hit = meta[pl.ds(index, 1), :] == wanted
        sel[g // nd, g % nd] = jnp.where(hit, 1.0, 0.0).astype(bf16)
        return carry

    lax.fori_loop(0, 2 * nd, build, 0)

    gate[...] = jnp.zeros_like(gate)
    upper[...] = jnp.zeros_like(upper)
    slots = nd * grp

    def select(e, i, slot, u):
        packed[e, i] = jnp.dot(
            sel[e].reshape(slots, nz * tok), held[i].reshape(nz * tok, LANES), preferred_element_type=f32
        ).astype(bf16).reshape(nd, grp, LANES)
        for r in range(1, nd):
            send(packed.at[e, i, r], rows.at[slot, u, r], x_send.at[e, i], x_recv.at[e, i], d_peer(r))
        rows[slot, u, 0] = packed[e, i, 0]

    def z_in(i):
        wait(held.at[i, pl.ds(1, nz - 1)], z_recv.at[i])

    def unit(v):
        e = v // late
        k = v % late
        return e, k, e * chunks + k

    def stage_a(v):
        e, k, u = unit(v)

        @pl.when(e == 0)
        def _():
            z_in(k)

        select(e, k, 0, u)

    def early_out(e, n):
        for slot in range(NY):
            i = late + NY * n + slot
            if e == 0:
                z_in(i)
            select(e, i, slot, e * chunks + late + n)

    def early_in(e, n):
        u = e * chunks + late + n
        for slot in range(NY):
            wait(rows.at[slot, u, pl.ds(1, nd - 1)], x_recv.at[e, late + NY * n + slot])
        accumulate(u, ((0, y), (1, left), (2, right), (3, across)))

    def stage_b(v):
        e, k, u = unit(v)
        wait(rows.at[0, u, pl.ds(1, nd - 1)], x_recv.at[e, k])
        send(rows.at[0, u], rows.at[1, u], y_send.at[0, u], y_recv.at[0, u], y_peer(right))
        send(rows.at[0, u], rows.at[2, u], y_send.at[1, u], y_recv.at[1, u], y_peer(left))

    halves = nd // 2
    first, second = pl.ds(0, halves), pl.ds(halves, halves)

    def accumulate(u, sources):
        e = u // chunks
        k = u % chunks

        def one(h, carry):
            g = gate[e, h]
            up = upper[e, h]
            for s, q in sources:
                x = rows[s, u, pl.ds(h * halves, halves)].reshape(halves * grp, LANES)
                at = pl.ds(pl.multiple_of(q * quarter + k * LANES, LANES), LANES)
                g = g + jnp.dot(x, wg[e, at, :], preferred_element_type=f32)
                up = up + jnp.dot(x, wu[e, at, :], preferred_element_type=f32)
            gate[e, h] = g
            upper[e, h] = up
            return carry

        lax.fori_loop(0, 2, one, 0)

    def stage_c(v):
        u = unit(v)[2]
        wait(rows.at[1, u], y_recv.at[0, u])
        send(rows.at[1, u, first], rows.at[3, u, first], y_send.at[2, u], y_recv.at[2, u], y_peer(right))
        wait(rows.at[2, u], y_recv.at[1, u])
        send(rows.at[2, u, second], rows.at[3, u, second], y_send.at[3, u], y_recv.at[3, u], y_peer(left))
        accumulate(u, ((0, y), (1, left), (2, right)))

    def stage_d(v):
        u = unit(v)[2]
        wait(rows.at[3, u, first], y_recv.at[2, u])
        wait(rows.at[3, u, second], y_recv.at[3, u])
        accumulate(u, ((3, across),))

    half_rows = halves * grp
    low, high = pl.ds(0, half_rows), pl.ds(half_rows, half_rows)
    units = 2 * chunks

    def hidden_out(e):
        for h in range(2):
            g = gate[e, h]
            hidden[0, e, h * half_rows:(h + 1) * half_rows, :] = (
                g / (1.0 + jnp.exp(-g)) * upper[e, h]
            ).astype(bf16)
        u = units + e
        send(hidden.at[0, e], hidden.at[1, e], y_send.at[0, u], y_recv.at[0, u], y_peer(right))
        send(hidden.at[0, e], hidden.at[2, e], y_send.at[1, u], y_recv.at[1, u], y_peer(left))

    def hidden_on(e):
        u = units + e
        wait(hidden.at[1, e], y_recv.at[0, u])
        send(hidden.at[1, e, low], hidden.at[3, e, low], y_send.at[2, u], y_recv.at[2, u], y_peer(right))
        wait(hidden.at[2, e], y_recv.at[1, u])
        send(hidden.at[2, e, high], hidden.at[3, e, high], y_send.at[3, u], y_recv.at[3, u], y_peer(left))

    def hidden_in(e):
        u = units + e
        wait(hidden.at[3, e, low], y_recv.at[2, u])
        wait(hidden.at[3, e, high], y_recv.at[3, u])

    def stage_e(e, k):
        cols = pl.ds(pl.multiple_of(k * LANES, LANES), LANES)
        total = jnp.zeros((slots, LANES), f32)
        for s in range(NY):
            total = total + jnp.dot(hidden[s, e], wd[s, e, :, cols], preferred_element_type=f32)
        value = total.astype(bf16).reshape(nd, grp, LANES)
        outs[e, k] = value
        back[e, k, 0] = value[0]
        for r in range(1, nd):
            send(outs.at[e, k, r], back.at[e, k, r], b_send.at[e, k], b_recv.at[e, k], d_peer(nd - r))

    def stage_f(e, k):
        wait(back.at[e, k, pl.ds(1, nd - 1)], b_recv.at[e, k])
        value = jnp.dot(
            order[...], back[e, k].reshape(slots, LANES), preferred_element_type=f32
        ).astype(bf16).reshape(nz, nd * cap, LANES)
        part[e, k] = value
        home[e, k, 0] = value[0]
        for j in range(1, nz):
            send(part.at[e, k, j], home.at[e, k, j], h_send.at[e, k], h_recv.at[e, k], z_peer(nz - j))

    def stage_g(k):
        @pl.when(k == 0)
        def _():
            for slot in (1, 2, 3):
                wait(pieces_y.at[slot - 1], p_recv.at[slot - 1])

        cols = pl.ds(pl.multiple_of(k * LANES, LANES), LANES)
        total = pieces[0, :, cols].astype(f32)
        for slot in (1, 2, 3):
            total = total + pieces_y[slot - 1, :, cols].astype(f32)
        for e in range(2):
            wait(home.at[e, k, pl.ds(1, nz - 1)], h_recv.at[e, k])
            total = total + jnp.dot(
                cmb[e], home[e, k].reshape(nz * nd * cap, LANES), preferred_element_type=f32
            )
        out_ref[:, cols] = total.astype(bf16)

    def build_return():
        at = lax.broadcasted_iota(jnp.int32, (slots, slots), 0)
        lane = lax.broadcasted_iota(jnp.int32, (1, slots), 1)
        source = lane % grp
        target = (source % nz) * (nd * cap) + source // nz * nd + (d + lane // grp) % nd
        order[...] = jnp.where(at == target, 1.0, 0.0).astype(bf16)

        for e in range(2):
            for j in range(nz):
                base = ((z + j) % nz) * plane + e
                ranks = score[0, pl.ds(base, nd, 2), :]
                weights = score[1, pl.ds(base, nd, 2), :]
                for p in range(cap):
                    at_row = (j * cap + p) * nd
                    turned[at_row:at_row + nd, :] = jnp.where(ranks == p, weights, 0.0)
            for a in range(nz * nd * cap // LANES):
                block = slice(a * LANES, (a + 1) * LANES)
                cmb[e, :, block] = turned[block, :].T.astype(bf16)

    def shards_in_plane():
        wait(shards.at[:, pl.ds(1, nz - 1), d], sz_recv)

    def send_shards(j):
        mine = shards.at[:, j, d]
        for r in range(1, nx):
            send(mine, mine, sx_send.at[r - 1], sx_recv.at[r - 1], (z * nd + ((x + r) % nx) * NC + core, y))
        send(mine, mine, sc_send.at[0], sc_recv.at[0], (z * nd + x * NC + 1 - core, y))

    def shards_in_chip():
        for r in range(1, nx):
            block = shards.at[:, :, d_of(r, core)]
            wait(block, sx_recv.at[r - 1])
            send(block, block, sc_send.at[r], sc_recv.at[r], (z * nd + x * NC + 1 - core, y))

    rp = shard_ref.shape[1]
    rs = quarter * NY // (nz * nd)
    per_quarter = quarter // rs
    run = min(per_quarter, nd)

    def spread_matrix():
        into = lax.broadcasted_iota(jnp.int32, spread.shape, 1)
        at = lax.broadcasted_iota(jnp.int32, spread.shape, 0)
        inner = into % rp
        spread[...] = jnp.where((inner < rs) & (at == into // rp * rs + inner), 1.0, 0.0).astype(bf16)

    def block_of(m, q, i):
        first = q * per_quarter + i * run
        zr = (z + nz - first // nd) % nz
        return shards[m, zr, pl.ds(first % nd, run)].reshape(run * rp, hid)

    def shared_expert():
        for r in range(nx):
            wait(shards.at[:, :, d_of(r, 1 - core)], sc_recv.at[r])
        s_gate = jnp.zeros((tok, hid), f32)
        s_upper = jnp.zeros((tok, hid), f32)
        for slot, q in ((0, y), (1, left), (2, right), (3, across)):
            if slot and not early:
                wait(tokens_y.at[slot - 1], t_recv.at[slot - 1])
            source = tokens_y[slot - 1] if slot else tokens_ref[...]
            padded[...] = jnp.dot(source, spread[...], preferred_element_type=f32).astype(bf16)
            for i in range(per_quarter // run):
                lhs = padded[:, i * run * rp:(i + 1) * run * rp]
                s_gate = s_gate + jnp.dot(lhs, block_of(0, q, i), preferred_element_type=f32)
                s_upper = s_upper + jnp.dot(lhs, block_of(1, q, i), preferred_element_type=f32)
        act = (s_gate / (1.0 + jnp.exp(-s_gate)) * s_upper).astype(bf16)
        across_rows = (((1,), (1,)), ((), ()))
        for slot, q in ((1, right), (2, left), (3, across), (0, y)):
            for i in range(per_quarter // run):
                padded[:, i * run * rp:(i + 1) * run * rp] = lax.dot_general(
                    act, block_of(2, q, i), across_rows, preferred_element_type=f32
                ).astype(bf16)
            pieces[slot] = lax.dot_general(
                padded[...], spread[...], across_rows, preferred_element_type=f32
            ).astype(bf16)

    def send_pieces():
        for slot, q in y_slots:
            send(pieces.at[slot], pieces_y.at[slot - 1], p_send.at[slot - 1], p_recv.at[slot - 1], y_peer(q))

    load_g.wait()
    load_u.wait()

    lag_b, lag_c, lag_d = 1, 2, 3

    def at_step(i, n, *calls):
        @pl.when(i == n)
        def _():
            for call in calls:
                call()

    def in_steps(i, low_step, high_step, call):
        @pl.when((i >= low_step) & (i < high_step))
        def _():
            call(i - low_step)

    def wd_in(e):
        for slot in (1, 2, 3):
            wait(wd.at[slot, e], wd_recv.at[slot - 1, e])

    def first_ready():
        load_d.wait()
        wd_in(0)
        hidden_in(0)

    def two(stage):
        def call(i):
            stage(0, 2 * i)

            @pl.when(2 * i + 1 < chunks)
            def _():
                stage(0, 2 * i + 1)

        return call

    ready = late - 1 + lag_d
    pairs = (chunks + 1) // 2
    v_end = 2 * late
    steps = v_end + lag_d
    plane_step = min(6, steps - 3)

    def two_shards(i):
        for j in range(2):
            send_shards(2 * i + j)

    def step(i, carry):
        in_steps(i, 0, v_end, stage_a)
        in_steps(i, lag_b, v_end + lag_b, stage_b)
        in_steps(i, 0, late - z_ahead, lambda k: send_late(k + z_ahead))
        in_steps(i, 0, units - wd_first, lambda u: send_wd(u + wd_first))
        at_step(i, 0, build_return)
        for n in range(early):
            at_step(i, late - z_ahead + n, functools.partial(send_early, n))
            at_step(i, ready - early + n, functools.partial(early_out, 0, n))
            at_step(i, ready + 1 + n, functools.partial(early_out, 1, n))
        at_step(i, 3, spread_matrix)
        at_step(i, min(late - z_ahead + early, plane_step), send_shard)
        at_step(i, plane_step, shards_in_plane)
        in_steps(i, plane_step, plane_step + nz // 2, two_shards)
        in_steps(i, lag_c, v_end + lag_c, stage_c)
        in_steps(i, lag_d, v_end + lag_d, stage_d)
        for n in range(early):
            at_step(i, ready - early + n + 1, functools.partial(early_in, 0, n))
            at_step(i, ready + 2 + n, functools.partial(early_in, 1, n))
        at_step(i, ready, lambda: hidden_out(0))
        at_step(i, ready + 1, lambda: hidden_on(0))
        at_step(i, ready + 2, first_ready)
        in_steps(i, ready + 2, ready + 2 + pairs, two(stage_e))
        in_steps(i, ready + 2, ready + 2 + pairs, two(stage_f))
        at_step(i, plane_step + nz // 2 + 1, shards_in_chip)
        at_step(i, steps - 1, shared_expert)
        return carry

    lax.fori_loop(0, steps, step, 0)

    hidden_out(1)
    hidden_on(1)
    send_pieces()
    hidden_in(1)
    wd_in(1)

    lag_f, lag_g = 1, 3

    def step_back(i, carry):
        @pl.when(i < chunks)
        def _():
            stage_e(1, i)

        @pl.when((i >= lag_f) & (i < chunks + lag_f))
        def _():
            stage_f(1, i - lag_f)

        @pl.when(i >= lag_g)
        def _():
            stage_g(i - lag_g)

        return carry

    lax.fori_loop(0, chunks + lag_g, step_back, 0)

    wait(meta.at[:, pl.ds(tok, (nz - 1) * tok)], meta_send)
    wait(shards.at[:, pl.ds(1, nz - 1), d], sz_send)
    for r in range(nx):
        if r:
            wait(shards.at[:, :, d], sx_send.at[r - 1])
        wait(shards.at[:, :, d_of(r, core)], sc_send.at[r])
    for slot in (1, 2, 3):
        wait(tokens_y.at[slot - 1], t_send.at[slot - 1])
        wait(pieces.at[slot], p_send.at[slot - 1])
        for e in range(2):
            wait(wd.at[slot, e], wd_send.at[slot - 1, e])

    def drain_parts(i, carry):
        wait(held.at[i, pl.ds(1, nz - 1)], z_send.at[i])
        for e in range(2):
            wait(packed.at[e, i, pl.ds(1, nd - 1)], x_send.at[e, i])
        return carry

    lax.fori_loop(0, parts, drain_parts, 0)

    def drain(k, carry):
        for e in range(2):
            wait(outs.at[e, k, pl.ds(1, nd - 1)], b_send.at[e, k])
            wait(part.at[e, k, pl.ds(1, nz - 1)], h_send.at[e, k])
        return carry

    lax.fori_loop(0, chunks, drain, 0)

    def drain_units(v, carry):
        u = unit(v)[2]
        wait(rows.at[0, u], y_send.at[0, u])
        wait(rows.at[0, u], y_send.at[1, u])
        wait(rows.at[1, u, first], y_send.at[2, u])
        wait(rows.at[2, u, second], y_send.at[3, u])
        return carry

    lax.fori_loop(0, v_end, drain_units, 0)
    for e in range(2):
        u = units + e
        wait(hidden.at[0, e], y_send.at[0, u])
        wait(hidden.at[0, e], y_send.at[1, u])
        wait(hidden.at[1, e, low], y_send.at[2, u])
        wait(hidden.at[2, e, high], y_send.at[3, u])


def layer(tokens, expert_ids, gate_weights, w_gate, w_up, w_down, shard, cap):
    nz, nx = dims_of(lax.axis_size("exp"))
    nd = nx * NC
    tok, quarter = tokens.shape
    top = expert_ids.shape[1]
    width, hid = w_gate.shape[1:]
    chunks = quarter // LANES
    grp = nz * cap
    f32, bf16 = jnp.float32, jnp.bfloat16
    dma = pltpu.SemaphoreType.DMA
    vm = pltpu.VMEM
    slots = 2 * nd * grp
    early = min(EARLY, chunks - 3)
    parts = chunks + (NY - 1) * early
    rp = shard.shape[1]
    padded_cols = quarter // (width // (nz * nd)) * rp
    hbm = pl.BlockSpec(memory_space=pl.ANY)
    inside = pl.BlockSpec(memory_space=pltpu.VMEM)
    return pl.pallas_call(
        functools.partial(layer_kernel, nz, nd, cap, tok, top, chunks, hid),
        out_shape=jax.ShapeDtypeStruct((tok, quarter), bf16),
        in_specs=[inside, inside, inside, hbm, hbm, hbm, inside],
        out_specs=inside,
        scratch_shapes=[
            vm((2, width, hid), bf16),
            vm((2, width, hid), bf16),
            vm((NY, 2, hid, quarter), bf16),
            vm((2, 2 * nz * nd, tok), f32),
            vm((2 * nd, nz * tok), f32),
            vm((2, nd, grp, nz * tok), bf16),
            vm((2, tok, nz * nd * cap), bf16),
            vm((nd * grp, nd * grp), bf16),
            vm((parts, nz, tok, LANES), bf16),
            vm((2, parts, nd, grp, LANES), bf16),
            vm((NY, 2 * chunks, nd, grp, LANES), bf16),
            vm((2, 2, nd // 2 * grp, hid), f32),
            vm((2, 2, nd // 2 * grp, hid), f32),
            vm((NY, 2, nd * grp, hid), bf16),
            vm((2, chunks, nd, grp, LANES), bf16),
            vm((2, chunks, nd, grp, LANES), bf16),
            vm((2, chunks, nz, nd * cap, LANES), bf16),
            vm((2, chunks, nz, nd * cap, LANES), bf16),
            vm((nz * nd * cap, tok), f32),
            vm((quarter, padded_cols), bf16),
            vm((3, nz, nd, rp, hid), bf16),
            vm((NY - 1, tok, quarter), bf16),
            vm((tok, padded_cols), bf16),
            vm((NY, tok, quarter), bf16),
            vm((NY - 1, tok, quarter), bf16),
            dma((3,)), dma((3, 2)), dma((3, 2)), dma, dma,
            dma((parts,)), dma((parts,)), dma((2, parts)), dma((2, parts)),
            dma((4, 2 * chunks + 2)), dma((4, 2 * chunks + 2)),
            dma((2, chunks)), dma((2, chunks)), dma((2, chunks)), dma((2, chunks)),
            dma, dma, dma((max(1, nx - 1),)), dma((max(1, nx - 1),)), dma((nx,)), dma((nx,)),
            dma((3,)), dma((3,)), dma((3,)), dma((3,)),
        ],
        compiler_params=pltpu.CompilerParams(
            collective_id=0, has_side_effects=True, vmem_limit_bytes=60 * 1024 * 1024
        ),
        cost_estimate=pl.CostEstimate(
            flops=2 * slots * width * hid * 3, bytes_accessed=6 * width * hid * 2, transcendentals=slots * hid
        ),
        name="layer",
    )(tokens, expert_ids.T, gate_weights.T, w_gate, w_up, w_down, shard)


def body(tokens, expert_ids, gate_weights, w_gate, w_up, w_down, s_gate, s_up, s_down):
    exp_count = lax.axis_size("exp")
    tok_count, top_count = expert_ids.shape
    experts = w_gate.shape[0] * exp_count
    capacity = max(2, 5 * tok_count * top_count // (4 * experts))
    rows = s_gate.shape[0]
    shard = jnp.stack([s_gate, s_up, s_down.T])
    shard = jnp.pad(shard, ((0, 0), (0, -rows % 64), (0, 0)))
    return layer(tokens, expert_ids, gate_weights, w_gate, w_up, w_down, shard, capacity)


def solution(mesh):
    return jax.shard_map(
        body,
        mesh=mesh,
        in_specs=(
            P("exp", "tp"),
            P("exp", None),
            P("exp", None),
            P("exp", None, "tp"),
            P("exp", None, "tp"),
            P("exp", "tp", None),
            P("exp", "tp"),
            P("exp", "tp"),
            P("tp", "exp"),
        ),
        out_specs=P("exp", "tp"),
        check_vma=False,
    )
```

```python
import functools

import jax
import jax.numpy as jnp
from jax import lax
from jax.experimental import pallas as pl
from jax.experimental.pallas import tpu as pltpu
from jax.sharding import PartitionSpec as P

MESH = pl.DeviceIdType.MESH
NY = 4
NC = 2
LANES = 128
EARLY = 0


def dims_of(exp_count):
    nz, nx = {64: (8, 4), 4: (2, 1)}[exp_count]
    return nz, nx


def layer_kernel(
    nz, nd, cap, tok, top, chunks, hid,
    tokens_ref, ids_ref, wts_ref, wg_hbm, wu_hbm, wd_hbm, shard_ref,
    out_ref,
    wg, wu, wd, score, meta, sel, cmb, order, held, packed, rows, gate, upper, hidden,
    outs, back, part, home, turned,
    spread, shards, tokens_y, padded, pieces, pieces_y, mixed,
    load_sem, wd_send, wd_recv, meta_send, meta_recv, z_send, z_recv, x_send, x_recv,
    y_send, y_recv, b_send, b_recv, h_send, h_recv,
    sz_send, sz_recv, sx_send, sx_recv, sc_send, sc_recv, t_send, t_recv, p_send, p_recv,
):
    quarter = chunks * LANES
    z_ahead = 3
    early = min(EARLY, chunks - 3)
    late = chunks - early
    parts = late + NY * early
    grp = nz * cap
    f32, bf16 = jnp.float32, jnp.bfloat16
    exp = lax.axis_index("exp")
    y = lax.axis_index("tp")
    z = exp // nd
    d = exp % nd
    right = (y + 1) % NY
    left = (y + NY - 1) % NY
    across = (y + 2) % NY

    def z_peer(j):
        return (((z + j) % nz) * nd + d, y)

    def d_peer(r):
        return (z * nd + (d + r) % nd, y)

    def y_peer(q):
        return (exp, q)

    nx = nd // NC
    x = d // NC
    core = d % NC

    def d_of(r, c):
        return ((x + nx - r) % nx) * NC + c

    def send(src, dst, ss, rs, dev):
        pltpu.make_async_remote_copy(
            src_ref=src, dst_ref=dst, send_sem=ss, recv_sem=rs, device_id=dev, device_id_type=MESH
        ).start()

    def wait(ref, sem):
        pltpu.make_async_copy(ref, ref, sem).wait()

    load_g = pltpu.make_async_copy(wg_hbm, wg, load_sem.at[0])
    load_u = pltpu.make_async_copy(wu_hbm, wu, load_sem.at[1])
    load_d = pltpu.make_async_copy(wd_hbm.at[:, :, pl.ds(y * quarter, quarter)], wd.at[0], load_sem.at[2])
    load_g.start()
    load_u.start()
    load_d.start()

    barrier = pltpu.get_barrier_semaphore()
    for j in range(1, nz):
        pl.semaphore_signal(barrier, inc=1, device_id=z_peer(j), device_id_type=MESH)
    for r in range(1, nd):
        pl.semaphore_signal(barrier, inc=1, device_id=d_peer(r), device_id_type=MESH)
    for q in (left, right, across):
        pl.semaphore_signal(barrier, inc=1, device_id=y_peer(q), device_id_type=MESH)

    experts = nz * nd * 2
    names = lax.broadcasted_iota(jnp.int32, (experts, tok), 0)
    named = jnp.zeros((experts, tok), f32)
    weight = jnp.zeros((experts, tok), f32)
    for k in range(top):
        hit = ids_ref[k:k + 1, :] == names
        named = named + jnp.where(hit, 1.0, 0.0)
        weight = weight + jnp.where(hit, wts_ref[k:k + 1, :], 0.0)
    before = lax.broadcasted_iota(jnp.int32, (tok, tok), 0) < lax.broadcasted_iota(jnp.int32, (tok, tok), 1)
    rank = jnp.dot(
        named.astype(bf16), jnp.where(before, 1.0, 0.0).astype(bf16), preferred_element_type=f32
    )
    score[0] = jnp.where(named > 0.5, rank, -1.0)
    score[1] = weight
    plane = 2 * nd

    pl.semaphore_wait(barrier, nz - 1 + nd - 1 + 3)

    for j in range(1, nz):
        zj = (z + j) % nz
        send(
            score.at[0, pl.ds(pl.multiple_of(zj * plane, plane), plane), :],
            meta.at[:, pl.ds(j * tok, tok)],
            meta_send, meta_recv, z_peer(j),
        )
    meta[:, 0:tok] = score[0, pl.ds(pl.multiple_of(z * plane, plane), plane), :]

    y_slots = ((1, right), (2, left), (3, across))

    def send_tokens(i, source, k):
        cols = pl.ds(pl.multiple_of(k * LANES, LANES), LANES)
        for j in range(1, nz):
            send(source.at[:, cols], held.at[i, j], z_send.at[i], z_recv.at[i], z_peer(j))
        held[i, 0] = source[:, cols]

    def send_late(k):
        send_tokens(k, tokens_ref, k)

    def send_early(n):
        if n == 0:
            for slot in (1, 2, 3):
                wait(tokens_y.at[slot - 1], t_recv.at[slot - 1])
        for slot in range(NY):
            source = tokens_y.at[slot - 1] if slot else tokens_ref
            send_tokens(late + NY * n + slot, source, late + n)

    def send_tokens_y():
        for slot, q in y_slots:
            send(tokens_ref, tokens_y.at[slot - 1], t_send.at[slot - 1], t_recv.at[slot - 1], y_peer(q))

    def send_wd(u):
        e = u // chunks
        k = u % chunks
        for slot, q in y_slots:
            send(
                wd_hbm.at[e, :, pl.ds(pl.multiple_of(q * quarter + k * LANES, LANES), LANES)],
                wd.at[slot, e, :, pl.ds(pl.multiple_of(k * LANES, LANES), LANES)],
                wd_send.at[slot - 1, e * (1 + k)], wd_recv.at[slot - 1, e * (1 + k)], y_peer(q),
            )

    def send_shard():
        for j in range(1, nz):
            send(shard_ref, shards.at[:, j, d], sz_send, sz_recv, z_peer(j))
        shards[:, 0, d] = shard_ref[...]

    send_late(0)
    send_tokens_y()
    for k in range(1, z_ahead):
        send_late(k)
    wd_first = min(4, chunks)
    wd_next = 2
    for u in range(wd_first):
        send_wd(u)

    wait(meta.at[:, pl.ds(tok, (nz - 1) * tok)], meta_recv)

    row = lax.broadcasted_iota(jnp.int32, (grp, nz * tok), 0)
    col = lax.broadcasted_iota(jnp.int32, (grp, nz * tok), 1)
    wanted = jnp.where(row % nz == col // tok, row // nz, -5).astype(f32)

    def build(g, carry):
        index = ((d + g % nd) % nd) * 2 + g // nd
        hit = meta[pl.ds(index, 1), :] == wanted
        sel[g // nd, g % nd] = jnp.where(hit, 1.0, 0.0).astype(bf16)
        return carry

    lax.fori_loop(0, nd, build, 0)

    gate[...] = jnp.zeros_like(gate)
    upper[...] = jnp.zeros_like(upper)
    slots = nd * grp

    def select(e, i, slot, u):
        packed[e, i] = jnp.dot(
            sel[e].reshape(slots, nz * tok), held[i].reshape(nz * tok, LANES), preferred_element_type=f32
        ).astype(bf16).reshape(nd, grp, LANES)
        for r in range(1, nd):
            send(packed.at[e, i, r], rows.at[slot, u, r], x_send.at[e, i], x_recv.at[e, i], d_peer(r))
        rows[slot, u, 0] = packed[e, i, 0]

    def z_in(i):
        wait(held.at[i, pl.ds(1, nz - 1)], z_recv.at[i])

    def unit(v):
        e = v // late
        k = v % late
        return e, k, e * chunks + k

    def stage_a(v):
        e, k, u = unit(v)

        @pl.when(e == 0)
        def _():
            z_in(k)

        select(e, k, 0, u)

    def early_out(e, n):
        for slot in range(NY):
            i = late + NY * n + slot
            if e == 0:
                z_in(i)
            select(e, i, slot, e * chunks + late + n)

    def early_in(e, n):
        u = e * chunks + late + n
        for slot in range(NY):
            wait(rows.at[slot, u, pl.ds(1, nd - 1)], x_recv.at[e, late + NY * n + slot])
        accumulate(u, ((0, y), (1, left), (2, right), (3, across)))

    def stage_b(v):
        e, k, u = unit(v)
        wait(rows.at[0, u, pl.ds(1, nd - 1)], x_recv.at[e, k])
        send(rows.at[0, u], rows.at[1, u], y_send.at[0, u], y_recv.at[0, u], y_peer(right))
        send(rows.at[0, u], rows.at[2, u], y_send.at[1, u], y_recv.at[1, u], y_peer(left))

    halves = nd // 2
    first, second = pl.ds(0, halves), pl.ds(halves, halves)

    def accumulate(u, sources):
        e = u // chunks
        k = u % chunks

        def one(h, carry):
            g = gate[e, h]
            up = upper[e, h]
            for s, q in sources:
                x = rows[s, u, pl.ds(h * halves, halves)].reshape(halves * grp, LANES)
                at = pl.ds(pl.multiple_of(q * quarter + k * LANES, LANES), LANES)
                g = g + jnp.dot(x, wg[e, at, :], preferred_element_type=f32)
                up = up + jnp.dot(x, wu[e, at, :], preferred_element_type=f32)
            gate[e, h] = g
            upper[e, h] = up
            return carry

        lax.fori_loop(0, 2, one, 0)

    def stage_c(v):
        u = unit(v)[2]
        wait(rows.at[1, u], y_recv.at[0, u])
        send(rows.at[1, u, first], rows.at[3, u, first], y_send.at[2, u], y_recv.at[2, u], y_peer(right))
        wait(rows.at[2, u], y_recv.at[1, u])
        send(rows.at[2, u, second], rows.at[3, u, second], y_send.at[3, u], y_recv.at[3, u], y_peer(left))
        accumulate(u, ((0, y), (1, left), (2, right)))

    def stage_d(v):
        u = unit(v)[2]
        wait(rows.at[3, u, first], y_recv.at[2, u])
        wait(rows.at[3, u, second], y_recv.at[3, u])
        accumulate(u, ((3, across),))

    half_rows = halves * grp
    low, high = pl.ds(0, half_rows), pl.ds(half_rows, half_rows)
    units = 2 * chunks

    def hidden_out(e):
        for h in range(2):
            g = gate[e, h]
            hidden[0, e, h * half_rows:(h + 1) * half_rows, :] = (
                g / (1.0 + jnp.exp(-g)) * upper[e, h]
            ).astype(bf16)
        u = units + e
        send(hidden.at[0, e], hidden.at[1, e], y_send.at[0, u], y_recv.at[0, u], y_peer(right))
        send(hidden.at[0, e], hidden.at[2, e], y_send.at[1, u], y_recv.at[1, u], y_peer(left))

    def hidden_on(e):
        u = units + e
        wait(hidden.at[1, e], y_recv.at[0, u])
        send(hidden.at[1, e, low], hidden.at[3, e, low], y_send.at[2, u], y_recv.at[2, u], y_peer(right))
        wait(hidden.at[2, e], y_recv.at[1, u])
        send(hidden.at[2, e, high], hidden.at[3, e, high], y_send.at[3, u], y_recv.at[3, u], y_peer(left))

    def hidden_in(e):
        u = units + e
        wait(hidden.at[3, e, low], y_recv.at[2, u])
        wait(hidden.at[3, e, high], y_recv.at[3, u])

    def stage_e(e, k):
        cols = pl.ds(pl.multiple_of(k * LANES, LANES), LANES)
        total = jnp.zeros((slots, LANES), f32)
        for s in range(NY):
            total = total + jnp.dot(hidden[s, e], wd[s, e, :, cols], preferred_element_type=f32)
        value = total.astype(bf16).reshape(nd, grp, LANES)
        outs[e, k] = value
        back[e, k, 0] = value[0]
        for r in range(1, nd):
            send(outs.at[e, k, r], back.at[e, k, r], b_send.at[e, k], b_recv.at[e, k], d_peer(nd - r))

    def stage_f(e, k):
        wait(back.at[e, k, pl.ds(1, nd - 1)], b_recv.at[e, k])
        value = jnp.dot(
            order[...], back[e, k].reshape(slots, LANES), preferred_element_type=f32
        ).astype(bf16).reshape(nz, nd * cap, LANES)
        part[e, k] = value
        home[e, k, 0] = value[0]
        for j in range(1, nz):
            send(part.at[e, k, j], home.at[e, k, j], h_send.at[e, k], h_recv.at[e, k], z_peer(nz - j))

    def stage_g(k):
        cols = pl.ds(pl.multiple_of(k * LANES, LANES), LANES)
        total = pieces[0, :, cols].astype(f32)
        for e in range(2):
            wait(home.at[e, k, pl.ds(1, nz - 1)], h_recv.at[e, k])
            total = total + jnp.dot(
                cmb[e], home[e, k].reshape(nz * nd * cap, LANES), preferred_element_type=f32
            )
        mixed[:, cols] = total

    def build_return():
        at = lax.broadcasted_iota(jnp.int32, (slots, slots), 0)
        lane = lax.broadcasted_iota(jnp.int32, (1, slots), 1)
        source = lane % grp
        target = (source % nz) * (nd * cap) + source // nz * nd + (d + lane // grp) % nd
        order[...] = jnp.where(at == target, 1.0, 0.0).astype(bf16)

        for e in range(2):
            for j in range(nz):
                base = ((z + j) % nz) * plane + e
                ranks = score[0, pl.ds(base, nd, 2), :]
                weights = score[1, pl.ds(base, nd, 2), :]
                for p in range(cap):
                    at_row = (j * cap + p) * nd
                    turned[at_row:at_row + nd, :] = jnp.where(ranks == p, weights, 0.0)
            for a in range(nz * nd * cap // LANES):
                block = slice(a * LANES, (a + 1) * LANES)
                cmb[e, :, block] = turned[block, :].T.astype(bf16)

    def shards_in_plane():
        wait(shards.at[:, pl.ds(1, nz - 1), d], sz_recv)

    def send_shards(j):
        mine = shards.at[:, j, d]
        for r in range(1, nx):
            send(mine, mine, sx_send.at[r - 1], sx_recv.at[r - 1], (z * nd + ((x + r) % nx) * NC + core, y))
        send(mine, mine, sc_send.at[0], sc_recv.at[0], (z * nd + x * NC + 1 - core, y))

    def shards_in_chip():
        for r in range(1, nx):
            block = shards.at[:, :, d_of(r, core)]
            wait(block, sx_recv.at[r - 1])
            send(block, block, sc_send.at[r], sc_recv.at[r], (z * nd + x * NC + 1 - core, y))

    rp = shard_ref.shape[1]
    rs = quarter * NY // (nz * nd)
    per_quarter = quarter // rs
    run = min(per_quarter, nd)

    def spread_matrix():
        into = lax.broadcasted_iota(jnp.int32, spread.shape, 1)
        at = lax.broadcasted_iota(jnp.int32, spread.shape, 0)
        inner = into % rp
        spread[...] = jnp.where((inner < rs) & (at == into // rp * rs + inner), 1.0, 0.0).astype(bf16)

    def block_of(m, q, i):
        first = q * per_quarter + i * run
        zr = (z + nz - first // nd) % nz
        return shards[m, zr, pl.ds(first % nd, run)].reshape(run * rp, hid)

    def shared_expert():
        for r in range(nx):
            wait(shards.at[:, :, d_of(r, 1 - core)], sc_recv.at[r])
        s_gate = jnp.zeros((tok, hid), f32)
        s_upper = jnp.zeros((tok, hid), f32)
        for slot, q in ((0, y), (1, left), (2, right), (3, across)):
            if slot and not early:
                wait(tokens_y.at[slot - 1], t_recv.at[slot - 1])
            source = tokens_y[slot - 1] if slot else tokens_ref[...]
            padded[...] = jnp.dot(source, spread[...], preferred_element_type=f32).astype(bf16)
            for i in range(per_quarter // run):
                lhs = padded[:, i * run * rp:(i + 1) * run * rp]
                s_gate = s_gate + jnp.dot(lhs, block_of(0, q, i), preferred_element_type=f32)
                s_upper = s_upper + jnp.dot(lhs, block_of(1, q, i), preferred_element_type=f32)
        act = (s_gate / (1.0 + jnp.exp(-s_gate)) * s_upper).astype(bf16)
        across_rows = (((1,), (1,)), ((), ()))
        for slot, q in ((1, right), (2, left), (3, across), (0, y)):
            for i in range(per_quarter // run):
                padded[:, i * run * rp:(i + 1) * run * rp] = lax.dot_general(
                    act, block_of(2, q, i), across_rows, preferred_element_type=f32
                ).astype(bf16)
            pieces[slot] = lax.dot_general(
                padded[...], spread[...], across_rows, preferred_element_type=f32
            ).astype(bf16)

    def send_pieces():
        for slot, q in y_slots:
            send(pieces.at[slot], pieces_y.at[slot - 1], p_send.at[slot - 1], p_recv.at[slot - 1], y_peer(q))

    load_g.wait()
    load_u.wait()

    lag_b, lag_c, lag_d = 2, 3, 4

    def at_step(i, n, *calls):
        @pl.when(i == n)
        def _():
            for call in calls:
                call()

    def in_steps(i, low_step, high_step, call):
        @pl.when((i >= low_step) & (i < high_step))
        def _():
            call(i - low_step)

    def wd_in(e, k):
        for slot in (1, 2, 3):
            if e == 0:
                wait(wd.at[slot, 0], wd_recv.at[slot - 1, 0])
            else:
                cols = pl.ds(pl.multiple_of(k * LANES, LANES), LANES)
                wait(wd.at[slot, 1, :, cols], wd_recv.at[slot - 1, 1 + k])

    def first_ready():
        load_d.wait()
        wd_in(0, 0)
        hidden_in(0)

    def two(stage):
        def call(i):
            stage(0, 2 * i)

            @pl.when(2 * i + 1 < chunks)
            def _():
                stage(0, 2 * i + 1)

        return call

    ready = late - 1 + lag_d
    pairs = (chunks + 1) // 2
    v_end = 2 * late
    steps = v_end + lag_d
    plane_step = min(6, steps - 3)

    def two_shards(i):
        send_shards(i)

    def step(i, carry):
        in_steps(i, 0, v_end, stage_a)
        in_steps(i, lag_b, v_end + lag_b, stage_b)
        in_steps(i, 0, late - z_ahead, lambda k: send_late(k + z_ahead))
        in_steps(i, 0, chunks + wd_next - wd_first, lambda u: send_wd(u + wd_first))
        at_step(i, 4, build_return)
        at_step(i, 1, lambda: lax.fori_loop(nd, 2 * nd, build, 0))
        for n in range(early):
            at_step(i, late - z_ahead + n, functools.partial(send_early, n))
            at_step(i, ready - early + n, functools.partial(early_out, 0, n))
            at_step(i, ready + 1 + n, functools.partial(early_out, 1, n))
        at_step(i, 3, spread_matrix)
        at_step(i, min(late - z_ahead + early, plane_step), send_shard)
        at_step(i, plane_step, shards_in_plane)
        in_steps(i, plane_step, plane_step + nz, two_shards)
        in_steps(i, lag_c, v_end + lag_c, stage_c)
        in_steps(i, lag_d, v_end + lag_d, stage_d)
        for n in range(early):
            at_step(i, ready - early + n + 1, functools.partial(early_in, 0, n))
            at_step(i, ready + 2 + n, functools.partial(early_in, 1, n))
        at_step(i, ready, lambda: hidden_out(0))
        at_step(i, ready + 1, lambda: hidden_on(0))
        at_step(i, ready + 2, first_ready)
        in_steps(i, ready + 2, ready + 2 + pairs, two(stage_e))
        in_steps(i, ready + 3, ready + 3 + pairs, two(stage_f))
        at_step(i, steps - 2, shards_in_chip)
        at_step(i, steps - 1, shared_expert)
        return carry

    lax.fori_loop(0, steps, step, 0)

    hidden_out(1)
    hidden_on(1)
    for k in range(wd_next, chunks):
        send_wd(chunks + k)
    send_pieces()
    for k in range(2 * min(pairs, max(0, steps - ready - 3)), chunks):
        stage_f(0, k)
    hidden_in(1)

    lag_f, lag_g = 1, 3

    def step_back(i, carry):
        @pl.when(i < chunks)
        def _():
            wd_in(1, i)
            stage_e(1, i)

        @pl.when((i >= lag_f) & (i < chunks + lag_f))
        def _():
            stage_f(1, i - lag_f)

        @pl.when(i >= lag_g)
        def _():
            stage_g(i - lag_g)

        return carry

    lax.fori_loop(0, chunks + lag_g, step_back, 0)

    for slot in (1, 2, 3):
        wait(pieces_y.at[slot - 1], p_recv.at[slot - 1])
    total = mixed[...]
    for slot in (1, 2, 3):
        total = total + pieces_y[slot - 1].astype(f32)
    out_ref[...] = total.astype(bf16)

    wait(meta.at[:, pl.ds(tok, (nz - 1) * tok)], meta_send)
    wait(shards.at[:, pl.ds(1, nz - 1), d], sz_send)
    for r in range(nx):
        if r:
            wait(shards.at[:, :, d], sx_send.at[r - 1])
        wait(shards.at[:, :, d_of(r, core)], sc_send.at[r])
    for slot in (1, 2, 3):
        wait(tokens_y.at[slot - 1], t_send.at[slot - 1])
        wait(pieces.at[slot], p_send.at[slot - 1])
        wait(wd.at[slot, 0], wd_send.at[slot - 1, 0])
        for k in range(chunks):
            wait(wd.at[slot, 1, :, pl.ds(k * LANES, LANES)], wd_send.at[slot - 1, 1 + k])

    def drain_parts(i, carry):
        wait(held.at[i, pl.ds(1, nz - 1)], z_send.at[i])
        for e in range(2):
            wait(packed.at[e, i, pl.ds(1, nd - 1)], x_send.at[e, i])
        return carry

    lax.fori_loop(0, parts, drain_parts, 0)

    def drain(k, carry):
        for e in range(2):
            wait(outs.at[e, k, pl.ds(1, nd - 1)], b_send.at[e, k])
            wait(part.at[e, k, pl.ds(1, nz - 1)], h_send.at[e, k])
        return carry

    lax.fori_loop(0, chunks, drain, 0)

    def drain_units(v, carry):
        u = unit(v)[2]
        wait(rows.at[0, u], y_send.at[0, u])
        wait(rows.at[0, u], y_send.at[1, u])
        wait(rows.at[1, u, first], y_send.at[2, u])
        wait(rows.at[2, u, second], y_send.at[3, u])
        return carry

    lax.fori_loop(0, v_end, drain_units, 0)
    for e in range(2):
        u = units + e
        wait(hidden.at[0, e], y_send.at[0, u])
        wait(hidden.at[0, e], y_send.at[1, u])
        wait(hidden.at[1, e, low], y_send.at[2, u])
        wait(hidden.at[2, e, high], y_send.at[3, u])


def layer(tokens, expert_ids, gate_weights, w_gate, w_up, w_down, shard, cap):
    nz, nx = dims_of(lax.axis_size("exp"))
    nd = nx * NC
    tok, quarter = tokens.shape
    top = expert_ids.shape[1]
    width, hid = w_gate.shape[1:]
    chunks = quarter // LANES
    grp = nz * cap
    f32, bf16 = jnp.float32, jnp.bfloat16
    dma = pltpu.SemaphoreType.DMA
    vm = pltpu.VMEM
    slots = 2 * nd * grp
    early = min(EARLY, chunks - 3)
    parts = chunks + (NY - 1) * early
    rp = shard.shape[1]
    padded_cols = quarter // (width // (nz * nd)) * rp
    hbm = pl.BlockSpec(memory_space=pl.ANY)
    inside = pl.BlockSpec(memory_space=pltpu.VMEM)
    return pl.pallas_call(
        functools.partial(layer_kernel, nz, nd, cap, tok, top, chunks, hid),
        out_shape=jax.ShapeDtypeStruct((tok, quarter), bf16),
        in_specs=[inside, inside, inside, hbm, hbm, hbm, inside],
        out_specs=inside,
        scratch_shapes=[
            vm((2, width, hid), bf16),
            vm((2, width, hid), bf16),
            vm((NY, 2, hid, quarter), bf16),
            vm((2, 2 * nz * nd, tok), f32),
            vm((2 * nd, nz * tok), f32),
            vm((2, nd, grp, nz * tok), bf16),
            vm((2, tok, nz * nd * cap), bf16),
            vm((nd * grp, nd * grp), bf16),
            vm((parts, nz, tok, LANES), bf16),
            vm((2, parts, nd, grp, LANES), bf16),
            vm((NY, 2 * chunks, nd, grp, LANES), bf16),
            vm((2, 2, nd // 2 * grp, hid), f32),
            vm((2, 2, nd // 2 * grp, hid), f32),
            vm((NY, 2, nd * grp, hid), bf16),
            vm((2, chunks, nd, grp, LANES), bf16),
            vm((2, chunks, nd, grp, LANES), bf16),
            vm((2, chunks, nz, nd * cap, LANES), bf16),
            vm((2, chunks, nz, nd * cap, LANES), bf16),
            vm((nz * nd * cap, tok), f32),
            vm((quarter, padded_cols), bf16),
            vm((3, nz, nd, rp, hid), bf16),
            vm((NY - 1, tok, quarter), bf16),
            vm((tok, padded_cols), bf16),
            vm((NY, tok, quarter), bf16),
            vm((NY - 1, tok, quarter), bf16),
            vm((tok, quarter), f32),
            dma((3,)), dma((3, chunks + 1)), dma((3, chunks + 1)), dma, dma,
            dma((parts,)), dma((parts,)), dma((2, parts)), dma((2, parts)),
            dma((4, 2 * chunks + 2)), dma((4, 2 * chunks + 2)),
            dma((2, chunks)), dma((2, chunks)), dma((2, chunks)), dma((2, chunks)),
            dma, dma, dma((max(1, nx - 1),)), dma((max(1, nx - 1),)), dma((nx,)), dma((nx,)),
            dma((3,)), dma((3,)), dma((3,)), dma((3,)),
        ],
        compiler_params=pltpu.CompilerParams(
            collective_id=0, has_side_effects=True, vmem_limit_bytes=60 * 1024 * 1024
        ),
        cost_estimate=pl.CostEstimate(
            flops=2 * slots * width * hid * 3, bytes_accessed=6 * width * hid * 2, transcendentals=slots * hid
        ),
        name="layer",
    )(tokens, expert_ids.T, gate_weights.T, w_gate, w_up, w_down, shard)


def body(tokens, expert_ids, gate_weights, w_gate, w_up, w_down, s_gate, s_up, s_down):
    exp_count = lax.axis_size("exp")
    tok_count, top_count = expert_ids.shape
    experts = w_gate.shape[0] * exp_count
    capacity = max(2, 5 * tok_count * top_count // (4 * experts))
    rows = s_gate.shape[0]
    shard = jnp.stack([s_gate, s_up, s_down.T])
    shard = jnp.pad(shard, ((0, 0), (0, -rows % 64), (0, 0)))
    return layer(tokens, expert_ids, gate_weights, w_gate, w_up, w_down, shard, capacity)


def solution(mesh):
    return jax.shard_map(
        body,
        mesh=mesh,
        in_specs=(
            P("exp", "tp"),
            P("exp", None),
            P("exp", None),
            P("exp", None, "tp"),
            P("exp", None, "tp"),
            P("exp", "tp", None),
            P("exp", "tp"),
            P("exp", "tp"),
            P("tp", "exp"),
        ),
        out_specs=P("exp", "tp"),
        check_vma=False,
    )
```

```python
import functools

import jax
import jax.numpy as jnp
from jax import lax
from jax.experimental import pallas as pl
from jax.experimental.pallas import tpu as pltpu
from jax.sharding import PartitionSpec as P

MESH = pl.DeviceIdType.MESH
NY = 4
NC = 2
LANES = 128
EARLY = 0


def dims_of(exp_count):
    nz, nx = {64: (8, 4), 4: (2, 1)}[exp_count]
    return nz, nx


def layer_kernel(
    nz, nd, cap, tok, top, chunks, hid,
    tokens_ref, ids_ref, wts_ref, wg_hbm, wu_hbm, wd_hbm, shard_ref,
    out_ref,
    wg, wu, wd, score, meta, sel, cmb, order, held, packed, rows, gate, upper, hidden,
    outs, back, part, home, turned,
    spread, shards, tokens_y, padded, pieces, pieces_y, mixed,
    load_sem, wd_send, wd_recv, meta_send, meta_recv, z_send, z_recv, x_send, x_recv,
    y_send, y_recv, b_send, b_recv, h_send, h_recv,
    sz_send, sz_recv, sx_send, sx_recv, sc_send, sc_recv, t_send, t_recv, p_send, p_recv,
):
    quarter = chunks * LANES
    z_ahead = 3
    early = min(EARLY, chunks - 3)
    late = chunks - early
    parts = late + NY * early
    grp = nz * cap
    f32, bf16 = jnp.float32, jnp.bfloat16
    exp = lax.axis_index("exp")
    y = lax.axis_index("tp")
    z = exp // nd
    d = exp % nd
    right = (y + 1) % NY
    left = (y + NY - 1) % NY
    across = (y + 2) % NY

    def z_peer(j):
        return (((z + j) % nz) * nd + d, y)

    def d_peer(r):
        return (z * nd + (d + r) % nd, y)

    def y_peer(q):
        return (exp, q)

    nx = nd // NC
    x = d // NC
    core = d % NC

    def d_of(r, c):
        return ((x + nx - r) % nx) * NC + c

    def send(src, dst, ss, rs, dev):
        pltpu.make_async_remote_copy(
            src_ref=src, dst_ref=dst, send_sem=ss, recv_sem=rs, device_id=dev, device_id_type=MESH
        ).start()

    def wait(ref, sem):
        pltpu.make_async_copy(ref, ref, sem).wait()

    load_g = pltpu.make_async_copy(wg_hbm, wg, load_sem.at[0])
    load_u = pltpu.make_async_copy(wu_hbm, wu, load_sem.at[1])
    load_d = pltpu.make_async_copy(wd_hbm.at[:, :, pl.ds(y * quarter, quarter)], wd.at[0], load_sem.at[2])
    load_g.start()
    load_u.start()
    load_d.start()

    barrier = pltpu.get_barrier_semaphore()
    for j in range(1, nz):
        pl.semaphore_signal(barrier, inc=1, device_id=z_peer(j), device_id_type=MESH)
    for r in range(1, nd):
        pl.semaphore_signal(barrier, inc=1, device_id=d_peer(r), device_id_type=MESH)
    for q in (left, right, across):
        pl.semaphore_signal(barrier, inc=1, device_id=y_peer(q), device_id_type=MESH)

    experts = nz * nd * 2
    names = lax.broadcasted_iota(jnp.int32, (experts, tok), 0)
    named = jnp.zeros((experts, tok), f32)
    weight = jnp.zeros((experts, tok), f32)
    for k in range(top):
        hit = ids_ref[k:k + 1, :] == names
        named = named + jnp.where(hit, 1.0, 0.0)
        weight = weight + jnp.where(hit, wts_ref[k:k + 1, :], 0.0)
    before = lax.broadcasted_iota(jnp.int32, (tok, tok), 0) < lax.broadcasted_iota(jnp.int32, (tok, tok), 1)
    rank = jnp.dot(
        named.astype(bf16), jnp.where(before, 1.0, 0.0).astype(bf16), preferred_element_type=f32
    )
    score[0] = jnp.where(named > 0.5, rank, -1.0)
    score[1] = weight
    plane = 2 * nd

    pl.semaphore_wait(barrier, nz - 1 + nd - 1 + 3)

    for j in range(1, nz):
        zj = (z + j) % nz
        send(
            score.at[0, pl.ds(pl.multiple_of(zj * plane, plane), plane), :],
            meta.at[:, pl.ds(j * tok, tok)],
            meta_send, meta_recv, z_peer(j),
        )
    meta[:, 0:tok] = score[0, pl.ds(pl.multiple_of(z * plane, plane), plane), :]

    y_slots = ((1, right), (2, left), (3, across))

    def send_tokens(i, source, k):
        cols = pl.ds(pl.multiple_of(k * LANES, LANES), LANES)
        for j in range(1, nz):
            send(source.at[:, cols], held.at[i, j], z_send.at[i], z_recv.at[i], z_peer(j))
        held[i, 0] = source[:, cols]

    def send_late(k):
        send_tokens(k, tokens_ref, k)

    def send_early(n):
        if n == 0:
            for slot in (1, 2, 3):
                wait(tokens_y.at[slot - 1], t_recv.at[slot - 1])
        for slot in range(NY):
            source = tokens_y.at[slot - 1] if slot else tokens_ref
            send_tokens(late + NY * n + slot, source, late + n)

    def send_tokens_y():
        for slot, q in y_slots:
            send(tokens_ref, tokens_y.at[slot - 1], t_send.at[slot - 1], t_recv.at[slot - 1], y_peer(q))

    def send_wd(u):
        e = u // chunks
        k = u % chunks
        for slot, q in y_slots:
            send(
                wd_hbm.at[e, :, pl.ds(pl.multiple_of(q * quarter + k * LANES, LANES), LANES)],
                wd.at[slot, e, :, pl.ds(pl.multiple_of(k * LANES, LANES), LANES)],
                wd_send.at[slot - 1, e * (1 + k)], wd_recv.at[slot - 1, e * (1 + k)], y_peer(q),
            )

    def send_shard():
        for j in range(1, nz):
            send(shard_ref, shards.at[:, j, d], sz_send, sz_recv, z_peer(j))
        shards[:, 0, d] = shard_ref[...]

    send_late(0)
    send_tokens_y()
    for k in range(1, z_ahead):
        send_late(k)
    wd_first = min(4, chunks)
    wd_next = 2
    for u in range(wd_first):
        send_wd(u)

    wait(meta.at[:, pl.ds(tok, (nz - 1) * tok)], meta_recv)

    row = lax.broadcasted_iota(jnp.int32, (grp, nz * tok), 0)
    col = lax.broadcasted_iota(jnp.int32, (grp, nz * tok), 1)
    wanted = jnp.where(row % nz == col // tok, row // nz, -5).astype(f32)

    def build(g, carry):
        index = ((d + g % nd) % nd) * 2 + g // nd
        hit = meta[pl.ds(index, 1), :] == wanted
        sel[g // nd, g % nd] = jnp.where(hit, 1.0, 0.0).astype(bf16)
        return carry

    lax.fori_loop(0, nd, build, 0)

    gate[...] = jnp.zeros_like(gate)
    upper[...] = jnp.zeros_like(upper)
    slots = nd * grp

    def select(e, i, slot, u):
        packed[e, i] = jnp.dot(
            sel[e].reshape(slots, nz * tok), held[i].reshape(nz * tok, LANES), preferred_element_type=f32
        ).astype(bf16).reshape(nd, grp, LANES)
        for r in range(1, nd):
            send(packed.at[e, i, r], rows.at[slot, u, r], x_send.at[e, i], x_recv.at[e, i], d_peer(r))
        rows[slot, u, 0] = packed[e, i, 0]

    def z_in(i):
        wait(held.at[i, pl.ds(1, nz - 1)], z_recv.at[i])

    def unit(v):
        e = v // late
        k = v % late
        return e, k, e * chunks + k

    def stage_a(v):
        e, k, u = unit(v)

        @pl.when(e == 0)
        def _():
            z_in(k)

        select(e, k, 0, u)

    def early_out(e, n):
        for slot in range(NY):
            i = late + NY * n + slot
            if e == 0:
                z_in(i)
            select(e, i, slot, e * chunks + late + n)

    def early_in(e, n):
        u = e * chunks + late + n
        for slot in range(NY):
            wait(rows.at[slot, u, pl.ds(1, nd - 1)], x_recv.at[e, late + NY * n + slot])
        accumulate(u, ((0, y), (1, left), (2, right), (3, across)))

    def stage_b(v):
        e, k, u = unit(v)
        wait(rows.at[0, u, pl.ds(1, nd - 1)], x_recv.at[e, k])
        send(rows.at[0, u], rows.at[1, u], y_send.at[0, u], y_recv.at[0, u], y_peer(right))
        send(rows.at[0, u], rows.at[2, u], y_send.at[1, u], y_recv.at[1, u], y_peer(left))

    halves = nd // 2
    first, second = pl.ds(0, halves), pl.ds(halves, halves)

    def accumulate(u, sources):
        e = u // chunks
        k = u % chunks

        def one(h, carry):
            g = gate[e, h]
            up = upper[e, h]
            for s, q in sources:
                x = rows[s, u, pl.ds(h * halves, halves)].reshape(halves * grp, LANES)
                at = pl.ds(pl.multiple_of(q * quarter + k * LANES, LANES), LANES)
                g = g + jnp.dot(x, wg[e, at, :], preferred_element_type=f32)
                up = up + jnp.dot(x, wu[e, at, :], preferred_element_type=f32)
            gate[e, h] = g
            upper[e, h] = up
            return carry

        lax.fori_loop(0, 2, one, 0)

    def stage_c(v):
        u = unit(v)[2]
        wait(rows.at[1, u], y_recv.at[0, u])
        send(rows.at[1, u, first], rows.at[3, u, first], y_send.at[2, u], y_recv.at[2, u], y_peer(right))
        wait(rows.at[2, u], y_recv.at[1, u])
        send(rows.at[2, u, second], rows.at[3, u, second], y_send.at[3, u], y_recv.at[3, u], y_peer(left))
        accumulate(u, ((0, y), (1, left), (2, right)))

    def stage_d(v):
        u = unit(v)[2]
        wait(rows.at[3, u, first], y_recv.at[2, u])
        wait(rows.at[3, u, second], y_recv.at[3, u])
        accumulate(u, ((3, across),))

    half_rows = halves * grp
    low, high = pl.ds(0, half_rows), pl.ds(half_rows, half_rows)
    units = 2 * chunks

    def hidden_out(e):
        for h in range(2):
            g = gate[e, h]
            hidden[0, e, h * half_rows:(h + 1) * half_rows, :] = (
                g / (1.0 + jnp.exp(-g)) * upper[e, h]
            ).astype(bf16)
        u = units + e
        send(hidden.at[0, e], hidden.at[1, e], y_send.at[0, u], y_recv.at[0, u], y_peer(right))
        send(hidden.at[0, e], hidden.at[2, e], y_send.at[1, u], y_recv.at[1, u], y_peer(left))

    def hidden_on(e):
        u = units + e
        wait(hidden.at[1, e], y_recv.at[0, u])
        send(hidden.at[1, e, low], hidden.at[3, e, low], y_send.at[2, u], y_recv.at[2, u], y_peer(right))
        wait(hidden.at[2, e], y_recv.at[1, u])
        send(hidden.at[2, e, high], hidden.at[3, e, high], y_send.at[3, u], y_recv.at[3, u], y_peer(left))

    def hidden_in(e):
        u = units + e
        wait(hidden.at[3, e, low], y_recv.at[2, u])
        wait(hidden.at[3, e, high], y_recv.at[3, u])

    def stage_e(e, k):
        cols = pl.ds(pl.multiple_of(k * LANES, LANES), LANES)
        total = jnp.zeros((slots, LANES), f32)
        for s in range(NY):
            total = total + jnp.dot(hidden[s, e], wd[s, e, :, cols], preferred_element_type=f32)
        value = total.astype(bf16).reshape(nd, grp, LANES)
        outs[e, k] = value
        back[e, k, 0] = value[0]
        for r in range(1, nd):
            send(outs.at[e, k, r], back.at[e, k, r], b_send.at[e, k], b_recv.at[e, k], d_peer(nd - r))

    def stage_f(e, k):
        wait(back.at[e, k, pl.ds(1, nd - 1)], b_recv.at[e, k])
        value = jnp.dot(
            order[...], back[e, k].reshape(slots, LANES), preferred_element_type=f32
        ).astype(bf16).reshape(nz, nd * cap, LANES)
        part[e, k] = value
        home[e, k, 0] = value[0]
        for j in range(1, nz):
            send(part.at[e, k, j], home.at[e, k, j], h_send.at[e, k], h_recv.at[e, k], z_peer(nz - j))

    def stage_g(k):
        cols = pl.ds(pl.multiple_of(k * LANES, LANES), LANES)
        total = pieces[0, :, cols].astype(f32)
        for e in range(2):
            wait(home.at[e, k, pl.ds(1, nz - 1)], h_recv.at[e, k])
            total = total + jnp.dot(
                cmb[e], home[e, k].reshape(nz * nd * cap, LANES), preferred_element_type=f32
            )
        mixed[:, cols] = total

    def build_return():
        at = lax.broadcasted_iota(jnp.int32, (slots, slots), 0)
        lane = lax.broadcasted_iota(jnp.int32, (1, slots), 1)
        source = lane % grp
        target = (source % nz) * (nd * cap) + source // nz * nd + (d + lane // grp) % nd
        order[...] = jnp.where(at == target, 1.0, 0.0).astype(bf16)

        for e in range(2):
            for j in range(nz):
                base = ((z + j) % nz) * plane + e
                ranks = score[0, pl.ds(base, nd, 2), :]
                weights = score[1, pl.ds(base, nd, 2), :]
                for p in range(cap):
                    at_row = (j * cap + p) * nd
                    turned[at_row:at_row + nd, :] = jnp.where(ranks == p, weights, 0.0)
            for a in range(nz * nd * cap // LANES):
                block = slice(a * LANES, (a + 1) * LANES)
                cmb[e, :, block] = turned[block, :].T.astype(bf16)

    def shards_in_plane():
        wait(shards.at[:, pl.ds(1, nz - 1), d], sz_recv)

    def send_shards(j):
        mine = shards.at[:, j, d]
        for r in range(1, nx):
            send(mine, mine, sx_send.at[r - 1], sx_recv.at[r - 1], (z * nd + ((x + r) % nx) * NC + core, y))
        send(mine, mine, sc_send.at[0], sc_recv.at[0], (z * nd + x * NC + 1 - core, y))

    def shards_in_chip():
        for r in range(1, nx):
            block = shards.at[:, :, d_of(r, core)]
            wait(block, sx_recv.at[r - 1])
            send(block, block, sc_send.at[r], sc_recv.at[r], (z * nd + x * NC + 1 - core, y))

    rp = shard_ref.shape[1]
    rs = quarter * NY // (nz * nd)
    per_quarter = quarter // rs
    run = min(per_quarter, nd)

    def spread_matrix():
        into = lax.broadcasted_iota(jnp.int32, spread.shape, 1)
        at = lax.broadcasted_iota(jnp.int32, spread.shape, 0)
        inner = into % rp
        spread[...] = jnp.where((inner < rs) & (at == into // rp * rs + inner), 1.0, 0.0).astype(bf16)

    def block_of(m, q, i):
        first = q * per_quarter + i * run
        zr = (z + nz - first // nd) % nz
        return shards[m, zr, pl.ds(first % nd, run)].reshape(run * rp, hid)

    def shared_expert():
        for r in range(nx):
            wait(shards.at[:, :, d_of(r, 1 - core)], sc_recv.at[r])
        s_gate = jnp.zeros((tok, hid), f32)
        s_upper = jnp.zeros((tok, hid), f32)
        for slot, q in ((0, y), (1, left), (2, right), (3, across)):
            if slot and not early:
                wait(tokens_y.at[slot - 1], t_recv.at[slot - 1])
            source = tokens_y[slot - 1] if slot else tokens_ref[...]
            padded[...] = jnp.dot(source, spread[...], preferred_element_type=f32).astype(bf16)
            for i in range(per_quarter // run):
                lhs = padded[:, i * run * rp:(i + 1) * run * rp]
                s_gate = s_gate + jnp.dot(lhs, block_of(0, q, i), preferred_element_type=f32)
                s_upper = s_upper + jnp.dot(lhs, block_of(1, q, i), preferred_element_type=f32)
        act = (s_gate / (1.0 + jnp.exp(-s_gate)) * s_upper).astype(bf16)
        across_rows = (((1,), (1,)), ((), ()))
        for slot, q in ((1, right), (2, left), (3, across), (0, y)):
            for i in range(per_quarter // run):
                padded[:, i * run * rp:(i + 1) * run * rp] = lax.dot_general(
                    act, block_of(2, q, i), across_rows, preferred_element_type=f32
                ).astype(bf16)
            pieces[slot] = lax.dot_general(
                padded[...], spread[...], across_rows, preferred_element_type=f32
            ).astype(bf16)

    def send_pieces():
        for slot, q in y_slots:
            send(pieces.at[slot], pieces_y.at[slot - 1], p_send.at[slot - 1], p_recv.at[slot - 1], y_peer(q))

    load_g.wait()
    load_u.wait()

    lag_b, lag_c, lag_d = 2, 3, 4

    def at_step(i, n, *calls):
        @pl.when(i == n)
        def _():
            for call in calls:
                call()

    def in_steps(i, low_step, high_step, call):
        @pl.when((i >= low_step) & (i < high_step))
        def _():
            call(i - low_step)

    def wd_in(e, k):
        for slot in (1, 2, 3):
            if e == 0:
                wait(wd.at[slot, 0], wd_recv.at[slot - 1, 0])
            else:
                cols = pl.ds(pl.multiple_of(k * LANES, LANES), LANES)
                wait(wd.at[slot, 1, :, cols], wd_recv.at[slot - 1, 1 + k])

    def first_ready():
        load_d.wait()
        wd_in(0, 0)
        hidden_in(0)

    def two(stage):
        def call(i):
            stage(0, 2 * i)

            @pl.when(2 * i + 1 < chunks)
            def _():
                stage(0, 2 * i + 1)

        return call

    ready = late - 1 + lag_d
    pairs = (chunks + 1) // 2
    v_end = 2 * late
    steps = v_end + lag_d
    plane_step = min(6, steps - 3)

    def two_shards(i):
        send_shards(i)

    def step(i, carry):
        in_steps(i, 0, v_end, stage_a)
        in_steps(i, lag_b, v_end + lag_b, stage_b)
        in_steps(i, 0, late - z_ahead, lambda k: send_late(k + z_ahead))
        in_steps(i, 0, chunks + wd_next - wd_first, lambda u: send_wd(u + wd_first))
        at_step(i, 4, build_return)
        at_step(i, 1, lambda: lax.fori_loop(nd, 2 * nd, build, 0))
        for n in range(early):
            at_step(i, late - z_ahead + n, functools.partial(send_early, n))
            at_step(i, ready - early + n, functools.partial(early_out, 0, n))
            at_step(i, ready + 1 + n, functools.partial(early_out, 1, n))
        at_step(i, 3, spread_matrix)
        at_step(i, min(late - z_ahead + early, plane_step), send_shard)
        at_step(i, plane_step, shards_in_plane)
        in_steps(i, plane_step, plane_step + nz, two_shards)
        in_steps(i, lag_c, v_end + lag_c, stage_c)
        in_steps(i, lag_d, v_end + lag_d, stage_d)
        for n in range(early):
            at_step(i, ready - early + n + 1, functools.partial(early_in, 0, n))
            at_step(i, ready + 2 + n, functools.partial(early_in, 1, n))
        at_step(i, ready, lambda: hidden_out(0))
        at_step(i, ready + 1, lambda: hidden_on(0))
        at_step(i, ready + 2, first_ready)
        in_steps(i, ready + 2, ready + 2 + pairs, two(stage_e))
        in_steps(i, ready + 3, ready + 3 + pairs, two(stage_f))
        at_step(i, steps - 2, shards_in_chip)
        at_step(i, steps - 1, shared_expert)
        return carry

    lax.fori_loop(0, steps, step, 0)

    hidden_out(1)
    hidden_on(1)
    for k in range(wd_next, chunks):
        send_wd(chunks + k)
    send_pieces()
    for k in range(2 * min(pairs, max(0, steps - ready - 3)), chunks):
        stage_f(0, k)
    hidden_in(1)

    lag_f, lag_g = 2, 5

    def step_back(i, carry):
        @pl.when(i < chunks)
        def _():
            wd_in(1, i)
            stage_e(1, i)

        @pl.when((i >= lag_f) & (i < chunks + lag_f))
        def _():
            stage_f(1, i - lag_f)

        @pl.when(i >= lag_g)
        def _():
            stage_g(i - lag_g)

        return carry

    lax.fori_loop(0, chunks + lag_g, step_back, 0)

    for slot in (1, 2, 3):
        wait(pieces_y.at[slot - 1], p_recv.at[slot - 1])
    total = mixed[...]
    for slot in (1, 2, 3):
        total = total + pieces_y[slot - 1].astype(f32)
    out_ref[...] = total.astype(bf16)

    wait(meta.at[:, pl.ds(tok, (nz - 1) * tok)], meta_send)
    wait(shards.at[:, pl.ds(1, nz - 1), d], sz_send)
    for r in range(nx):
        if r:
            wait(shards.at[:, :, d], sx_send.at[r - 1])
        wait(shards.at[:, :, d_of(r, core)], sc_send.at[r])
    for slot in (1, 2, 3):
        wait(tokens_y.at[slot - 1], t_send.at[slot - 1])
        wait(pieces.at[slot], p_send.at[slot - 1])
        wait(wd.at[slot, 0], wd_send.at[slot - 1, 0])
        for k in range(chunks):
            wait(wd.at[slot, 1, :, pl.ds(k * LANES, LANES)], wd_send.at[slot - 1, 1 + k])

    def drain_parts(i, carry):
        wait(held.at[i, pl.ds(1, nz - 1)], z_send.at[i])
        for e in range(2):
            wait(packed.at[e, i, pl.ds(1, nd - 1)], x_send.at[e, i])
        return carry

    lax.fori_loop(0, parts, drain_parts, 0)

    def drain(k, carry):
        for e in range(2):
            wait(outs.at[e, k, pl.ds(1, nd - 1)], b_send.at[e, k])
            wait(part.at[e, k, pl.ds(1, nz - 1)], h_send.at[e, k])
        return carry

    lax.fori_loop(0, chunks, drain, 0)

    def drain_units(v, carry):
        u = unit(v)[2]
        wait(rows.at[0, u], y_send.at[0, u])
        wait(rows.at[0, u], y_send.at[1, u])
        wait(rows.at[1, u, first], y_send.at[2, u])
        wait(rows.at[2, u, second], y_send.at[3, u])
        return carry

    lax.fori_loop(0, v_end, drain_units, 0)
    for e in range(2):
        u = units + e
        wait(hidden.at[0, e], y_send.at[0, u])
        wait(hidden.at[0, e], y_send.at[1, u])
        wait(hidden.at[1, e, low], y_send.at[2, u])
        wait(hidden.at[2, e, high], y_send.at[3, u])


def layer(tokens, expert_ids, gate_weights, w_gate, w_up, w_down, shard, cap):
    nz, nx = dims_of(lax.axis_size("exp"))
    nd = nx * NC
    tok, quarter = tokens.shape
    top = expert_ids.shape[1]
    width, hid = w_gate.shape[1:]
    chunks = quarter // LANES
    grp = nz * cap
    f32, bf16 = jnp.float32, jnp.bfloat16
    dma = pltpu.SemaphoreType.DMA
    vm = pltpu.VMEM
    slots = 2 * nd * grp
    early = min(EARLY, chunks - 3)
    parts = chunks + (NY - 1) * early
    rp = shard.shape[1]
    padded_cols = quarter // (width // (nz * nd)) * rp
    hbm = pl.BlockSpec(memory_space=pl.ANY)
    inside = pl.BlockSpec(memory_space=pltpu.VMEM)
    return pl.pallas_call(
        functools.partial(layer_kernel, nz, nd, cap, tok, top, chunks, hid),
        out_shape=jax.ShapeDtypeStruct((tok, quarter), bf16),
        in_specs=[inside, inside, inside, hbm, hbm, hbm, inside],
        out_specs=inside,
        scratch_shapes=[
            vm((2, width, hid), bf16),
            vm((2, width, hid), bf16),
            vm((NY, 2, hid, quarter), bf16),
            vm((2, 2 * nz * nd, tok), f32),
            vm((2 * nd, nz * tok), f32),
            vm((2, nd, grp, nz * tok), bf16),
            vm((2, tok, nz * nd * cap), bf16),
            vm((nd * grp, nd * grp), bf16),
            vm((parts, nz, tok, LANES), bf16),
            vm((2, parts, nd, grp, LANES), bf16),
            vm((NY, 2 * chunks, nd, grp, LANES), bf16),
            vm((2, 2, nd // 2 * grp, hid), f32),
            vm((2, 2, nd // 2 * grp, hid), f32),
            vm((NY, 2, nd * grp, hid), bf16),
            vm((2, chunks, nd, grp, LANES), bf16),
            vm((2, chunks, nd, grp, LANES), bf16),
            vm((2, chunks, nz, nd * cap, LANES), bf16),
            vm((2, chunks, nz, nd * cap, LANES), bf16),
            vm((nz * nd * cap, tok), f32),
            vm((quarter, padded_cols), bf16),
            vm((3, nz, nd, rp, hid), bf16),
            vm((NY - 1, tok, quarter), bf16),
            vm((tok, padded_cols), bf16),
            vm((NY, tok, quarter), bf16),
            vm((NY - 1, tok, quarter), bf16),
            vm((tok, quarter), f32),
            dma((3,)), dma((3, chunks + 1)), dma((3, chunks + 1)), dma, dma,
            dma((parts,)), dma((parts,)), dma((2, parts)), dma((2, parts)),
            dma((4, 2 * chunks + 2)), dma((4, 2 * chunks + 2)),
            dma((2, chunks)), dma((2, chunks)), dma((2, chunks)), dma((2, chunks)),
            dma, dma, dma((max(1, nx - 1),)), dma((max(1, nx - 1),)), dma((nx,)), dma((nx,)),
            dma((3,)), dma((3,)), dma((3,)), dma((3,)),
        ],
        compiler_params=pltpu.CompilerParams(
            collective_id=0, has_side_effects=True, vmem_limit_bytes=60 * 1024 * 1024
        ),
        cost_estimate=pl.CostEstimate(
            flops=2 * slots * width * hid * 3, bytes_accessed=6 * width * hid * 2, transcendentals=slots * hid
        ),
        name="layer",
    )(tokens, expert_ids.T, gate_weights.T, w_gate, w_up, w_down, shard)


def body(tokens, expert_ids, gate_weights, w_gate, w_up, w_down, s_gate, s_up, s_down):
    exp_count = lax.axis_size("exp")
    tok_count, top_count = expert_ids.shape
    experts = w_gate.shape[0] * exp_count
    capacity = max(2, 5 * tok_count * top_count // (4 * experts))
    rows = s_gate.shape[0]
    shard = jnp.stack([s_gate, s_up, s_down.T])
    shard = jnp.pad(shard, ((0, 0), (0, -rows % 64), (0, 0)))
    return layer(tokens, expert_ids, gate_weights, w_gate, w_up, w_down, shard, capacity)


def solution(mesh):
    return jax.shard_map(
        body,
        mesh=mesh,
        in_specs=(
            P("exp", "tp"),
            P("exp", None),
            P("exp", None),
            P("exp", None, "tp"),
            P("exp", None, "tp"),
            P("exp", "tp", None),
            P("exp", "tp"),
            P("exp", "tp"),
            P("tp", "exp"),
        ),
        out_specs=P("exp", "tp"),
        check_vma=False,
    )
```
